32 devices in a mesh: store: 4 (over z), mp: 8 (over y, x, core).
Axes of the slice: x: 2, y: 2, z: 4, core: 2. Of those that a mesh axis runs over, the one named last changes fastest.
Arguments:
- tokens: bfloat16 [1024, 6144], P('store', 'mp'), may hold values from -6 to 6
- gain: float32 [6144], replicated, may hold values from 0.1 to 1.9
- base_projection_weight: bfloat16 [6144, 6144], P(None, 'mp'), may hold values from -0.078125 to 0.078125
- adapter_down_weight: bfloat16 [32, 64, 6144], P('store', None, 'mp'), may hold values from -0.078125 to 0.078125
- adapter_up_weight: bfloat16 [32, 64, 6144], P('store', None, 'mp'), may hold values from -0.75 to 0.75
- plan: int32 [4, 4], replicated, may hold values from 0 to 31, as said below
- target: int32 [1024, 1], P('store'), may hold values from 0 to 3; in each aligned block of 256 rows (0 to 255, 256 to 511, ...) at most 64 rows name the same one
- slot: int32 [1024], P('store'), may hold values from 0 to 11
Outputs:
- hidden_out: bfloat16 [1024, 6144], P('store', 'mp')
The draws below stay inside these ranges and needn't reach their ends.
Inputs may be any that keep to these rules, and one draw needn't show every extreme that they name: plan[g, r] is an adapter owned by a store group other than g; adapter a is owned by group a // 8. `target`: among the 256 rows of one store group at most 64 name the same group, a bound that some block reaches.
All inputs are finite; a program needn't handle non-finite values.
Results may differ from the reference program's by a relative error of at most 0.0063.
Values may be sent and summed in bfloat16 or wider, within the bound.
No kernel may reach another device: no remote copies, remote signals or barrier semaphores. Data moves between devices by JAX's collectives and lax.ppermute only.
A program may use at most 64 MiB of HBM per device.

```python
import math
import jax
import jax.numpy as jnp
import numpy as np
from jax import lax

MODEL_WIDTH = 6144
ADAPTER_RANK = 64
STEPS = 4
REPL = 4
ADP_GRP = 8
TOK_GRP = 256
CAP = 64
SLOTS = 12
ADAPTER_TOTAL = 32
TOKENS = 1024
N_STORE = 4


def draw_plan(key, part):
    groups = ADAPTER_TOTAL // ADP_GRP
    first_key = jax.random.fold_in(key, 11)
    second_key = jax.random.fold_in(key, 23)
    offset = jax.random.randint(first_key, (groups, REPL), 0, groups - 1)
    local = jax.random.randint(second_key, (groups, REPL), 0, ADP_GRP)
    owner = (jnp.arange(groups, dtype=jnp.int32)[:, None] + 1 + offset) % groups
    return (owner * ADP_GRP + local).astype(jnp.int32)


def plant(array, rng, least, high):
    extent = array.shape
    place = [jax.random.randint(jax.random.fold_in(rng, axis), (), 0, extent[axis]) for axis in range(len(extent))]
    array = array.at[tuple(place)].set(least)
    longest = extent.index(max(extent))
    place[longest] = (place[longest] + 1) % extent[longest]
    return array.at[tuple(place)].set(high)


def block_levels(rng, dims, pieces, least, top_value):
    factor_of = 1.0
    for dim, blocks in pieces:
        steps = jax.random.uniform(jax.random.fold_in(jax.random.fold_in(rng, 6), dim), (blocks,), jnp.float32, least / len(pieces), top_value / len(pieces))
        factor_of = factor_of * jnp.repeat(jnp.exp(steps), dims[dim] // blocks).reshape((-1,) + (1,) * (len(dims) - 1 - dim))
    return factor_of


def routed_block(key, own, number, rows, amount, top, reach, slope):
    order = jax.random.permutation(key, amount)
    packed, common = load_shares(amount, rows * top, reach, slope, True), load_shares(amount, rows * top, reach, slope, False)
    places = jnp.arange(amount)

    def named(tallies, rotation):
        used = int((tallies > 0).sum())
        fixed = max(1, used // 4)
        passed = fixed + (places - fixed + rotation * (used - fixed)) % max(1, amount - fixed)
        return jnp.zeros((amount,), jnp.int32).at[order[jnp.where(places < fixed, places, passed)]].set(jnp.asarray(tallies, jnp.int32))

    tallies = jnp.where(number % 4 == 0, named(packed, number // 4), named(common, number - number // 4 - 1))
    mixed = jax.random.permutation(jax.random.fold_in(own, 3), amount)
    donor, sink = mixed[0:amount // 2 * 2:2], mixed[1:amount // 2 * 2:2]
    margin = jnp.minimum(tallies[donor] - 1, reach - tallies[sink]) // 2
    margin = jnp.where((donor == order[0]) | (sink == order[0]) | (tallies[sink] == 0), 0, jnp.maximum(margin, 0))
    passed = jax.random.randint(jax.random.fold_in(own, 4), (amount // 2,), 0, 1 << 20) % (margin + 1)
    tallies = tallies.at[donor].add(-passed).at[sink].add(passed)
    members = jnp.searchsorted(jnp.cumsum(tallies), jnp.arange(rows * top), side="right").astype(jnp.int32)
    grid = members.reshape(top, rows).T
    grid = grid[jax.random.permutation(jax.random.fold_in(own, 1), rows)]
    rotation = jax.random.randint(jax.random.fold_in(own, 2), (rows, 1), 0, top)
    return jnp.take_along_axis(grid, (jnp.arange(top)[None, :] + rotation) % top, axis=1)


def load_shares(number_of, total, bound, slope, full):
    weights = [(1 << 20) // math.isqrt(rank ** slope) + 1 for rank in range(1, number_of + 1)]
    largest = bound if full else min(bound, max(-(-total // number_of), total * weights[0] // sum(weights)))
    least = 1 if total - largest >= number_of - 1 else 0
    holding, surplus = [largest] + [least] * (number_of - 1), total - largest - least * (number_of - 1)
    while surplus > 0:
        free = [i for i in range(1, number_of) if holding[i] < largest] or [i for i in range(1, number_of) if holding[i] < bound]
        pool, budget = sum([weights[i] for i in free]), surplus
        for i in free:
            addition = min(bound - holding[i], max(1, budget * weights[i] // pool), surplus)
            holding[i] = holding[i] + addition
            surplus = surplus - addition
    return np.array(holding)


def normal_values(own_key, shape, scale, bound, cuts=(), kind=jnp.bfloat16):
    drawn = jax.random.normal(own_key, shape, jnp.float32) * scale
    if len(cuts) > 0:
        drawn = block_levels(own_key, shape, cuts, -0.22, 0.18) * drawn
    return jnp.clip(drawn, min=-bound, max=bound).astype(kind)


def setup_inputs(seed: int = 0) -> dict:
    streams_of = jax.random.split(jax.random.key(seed), 9)
    tokens = normal_values(streams_of[0], (TOKENS, MODEL_WIDTH), 1.0, 6.0, ((0, 4), (1, 8)))
    gain = jnp.clip(1.0 + 0.18 * jax.random.normal(streams_of[1], (MODEL_WIDTH,), jnp.float32), 0.1, 1.9)
    base_projection_weight = normal_values(streams_of[2], (MODEL_WIDTH, MODEL_WIDTH), MODEL_WIDTH ** -0.5, 0.078125, ((1, 8),))
    adapter_down_weight = normal_values(streams_of[3], (ADAPTER_TOTAL, ADAPTER_RANK, MODEL_WIDTH), MODEL_WIDTH ** -0.5, 0.078125, ((0, 4), (2, 8)))
    adapter_up_weight = normal_values(streams_of[4], (ADAPTER_TOTAL, ADAPTER_RANK, MODEL_WIDTH), ADAPTER_RANK ** -0.5, 0.75, ((0, 4), (2, 8)))
    plan = draw_plan(jax.random.fold_in(streams_of[8], 71), 0)
    target_keys = jax.random.split(jax.random.fold_in(streams_of[6], 1), TOKENS // TOK_GRP)
    target_turns = jax.random.permutation(jax.random.fold_in(streams_of[6], 3), TOKENS // TOK_GRP)
    target = jax.vmap(lambda own, number: routed_block(jax.random.fold_in(streams_of[6], 2), own, number, TOK_GRP, N_STORE, 1, CAP, 2))(target_keys, target_turns).reshape((TOKENS, 1))
    slot = plant(jax.random.randint(streams_of[7], (TOKENS,), 0, SLOTS), jax.random.fold_in(streams_of[7], 1), 0, SLOTS - 1).astype(jnp.int32)
    return dict(tokens=tokens, gain=gain, base_projection_weight=base_projection_weight, adapter_down_weight=adapter_down_weight, adapter_up_weight=adapter_up_weight, plan=plan, target=target, slot=slot)


adapter_scale = 0.5

def reference(tokens, gain, base_projection_weight, adapter_down_weight, adapter_up_weight, plan, target, slot):
    target_group = target[:, 0].astype(jnp.int32)
    copy_index = jnp.clip(slot - ADP_GRP, 0, REPL - 1).astype(jnp.int32)
    adapter = jnp.where(slot < ADP_GRP, target_group * ADP_GRP + slot, plan[target_group, copy_index]).astype(jnp.int32)
    state = tokens
    for step in range(STEPS):
        values = state.astype(jnp.float32)
        mean_sq = lax.optimization_barrier(jnp.mean(values * values, axis=1, keepdims=True))
        normed = (values * lax.rsqrt(mean_sq + 1e-05) * gain.astype(jnp.float32)[None, :]).astype(jnp.bfloat16)
        base = jnp.dot(normed, base_projection_weight, preferred_element_type=jnp.float32)

        def block_work(pair):
            rows, selected_adapter = pair
            input_factor = adapter_down_weight[selected_adapter].astype(jnp.float32)
            inner = jnp.einsum('tk,trk->tr', rows.astype(jnp.float32), input_factor).astype(jnp.bfloat16)
            output_factor = adapter_up_weight[selected_adapter].astype(jnp.float32)
            outer = jnp.einsum('tr,trk->tk', inner.astype(jnp.float32), output_factor)
            return (adapter_scale * outer).astype(jnp.bfloat16)
        delta = lax.map(block_work, (normed.reshape(-1, CAP, MODEL_WIDTH), adapter.reshape(-1, CAP))).reshape(TOKENS, MODEL_WIDTH)
        state = (values + base + delta.astype(jnp.float32)).astype(jnp.bfloat16)
    return state
```

```python
import functools
import math

import jax
import jax.numpy as jnp
from jax import lax
from jax.experimental import pallas as pl
from jax.experimental.pallas import tpu as pltpu
from jax.sharding import PartitionSpec as P

STEPS = 4
CAP = 64
EPS = 1e-05
EXT = 16
MIB = 2**20

adapter_scale = 0.5

F32 = jnp.float32
BF16 = jnp.bfloat16
IN_VMEM = pl.BlockSpec(memory_space=pltpu.VMEM)
IN_SMEM = pl.BlockSpec(memory_space=pltpu.SMEM)
CONTRACT_LAST = (((1,), (1,)), ((), ()))
CONTRACT_FIRST = (((0,), (0,)), ((), ()))


def call(kernel, out, specs, *args, flops=0, name=None):
    many = isinstance(out, list)
    shapes = [jax.ShapeDtypeStruct(s, d) for s, d in (out if many else [out])]
    moved = sum(a.size * a.dtype.itemsize for a in args if a.size < 2**20)
    r = pl.pallas_call(
        kernel,
        out_shape=shapes,
        in_specs=specs,
        out_specs=[IN_VMEM] * len(shapes),
        compiler_params=pltpu.CompilerParams(vmem_limit_bytes=24 * MIB),
        cost_estimate=pl.CostEstimate(flops=flops, bytes_accessed=moved, transcendentals=0),
        name=name,
    )(*args)
    return r if many else r[0]


def dot(a, b, dims=(((1,), (0,)), ((), ()))):
    return lax.dot_general(a, b, dims, preferred_element_type=F32)


def iota(shape, dim):
    return lax.broadcasted_iota(jnp.int32, shape, dim)


def sort_kernel(me_ref, tokens_ref, target_ref, slot_ref, perm_ref, *chunk_refs):
    n_tokens, width = tokens_ref.shape
    groups = len(chunk_refs)
    rows = groups * CAP
    apart = jnp.bitwise_xor(target_ref[...], me_ref[0])
    member = (iota((max(8, groups), n_tokens), 0) == apart).astype(F32)
    before = (iota((n_tokens, n_tokens), 0) < iota((n_tokens, n_tokens), 1)).astype(BF16)
    earlier = dot(member.astype(BF16), before)
    place = jnp.sum(earlier * member, axis=0, keepdims=True).astype(jnp.int32)
    perm = (iota((rows, n_tokens), 0) == apart * CAP + place).astype(F32).astype(BF16)
    perm_ref[...] = perm
    sorted_rows = dot(perm, tokens_ref[...]).astype(BF16)
    slots = jnp.broadcast_to((slot_ref[...] + 1).astype(F32), (8, n_tokens)).astype(BF16)
    slots = dot(slots, perm, CONTRACT_LAST)
    lanes = 2 * CAP
    for k, ref in enumerate(chunk_refs):
        ref[:, :width] = sorted_rows[k * CAP : (k + 1) * CAP]
        half = slots[:, (k // 2) * lanes : (k // 2 + 1) * lanes]
        ref[:, width:] = jnp.concatenate([half, jnp.zeros((CAP - 8, lanes), F32)], 0).astype(BF16)


def unsort_kernel(perm_ref, *refs):
    rows = jnp.concatenate([r[...] for r in refs[:-1]], axis=0)
    refs[-1][...] = dot(perm_ref[...], rows, CONTRACT_FIRST).astype(BF16)


def pick_kernel(owned, where_ref, plan_ref, own_ref, carry_ref, out_ref):
    rank = own_ref.shape[0] // owned
    for r in range(plan_ref.shape[1]):
        adapter = plan_ref[where_ref[1], r]
        mine = adapter // owned == where_ref[0]
        at = slice(r * rank, (r + 1) * rank)

        @pl.when(mine)
        def _():
            out_ref[at, :] = own_ref[pl.ds((adapter % owned) * rank, rank), :]

        @pl.when(jnp.logical_not(mine))
        def _():
            out_ref[at, :] = carry_ref[at, :]


def fetch_copies(plan, own, owned, group, groups):
    copies = plan.shape[1]
    rank = own[0].shape[0] // owned
    zero = jnp.zeros((copies * rank, own[0].shape[1]), BF16)
    up, down = [zero] * len(own), [zero] * len(own)
    for r in range(1, groups):
        for i, factor in enumerate(own):
            for carry, step in ((up, 1), (down, -1)):
                place = group if step > 0 else groups - 1 - group
                dest = jnp.clip(groups + place - r, 0, groups - 1)
                dest = dest if step > 0 else groups - 1 - dest
                send = call(
                    functools.partial(pick_kernel, owned),
                    (zero.shape, BF16),
                    [IN_SMEM, IN_SMEM, IN_VMEM, IN_VMEM],
                    jnp.stack([group, dest]).astype(jnp.int32),
                    plan,
                    factor,
                    carry[i],
                    name="pick",
                )
                chain = [(g, g + 1) for g in range(r)]
                if step < 0:
                    chain = [(groups - 1 - a, groups - 1 - b) for a, b in chain]
                carry[i] = lax.ppermute(send, "store", chain)
    return [a + b for a, b in zip(up, down)]


def two_parts(row):
    high = row.astype(BF16).astype(F32)
    at = iota((EXT, row.shape[1]), 0)
    return jnp.where(at == 0, high, jnp.where(at == 1, row - high, 0.0)).astype(BF16)


def put_extra(msg_ref, rows, inner, squares):
    width = msg_ref.shape[1]
    groups = 0 if inner is None else inner.shape[0] // EXT
    rank_groups = width // rows
    msg_ref[rows:, :] = jnp.zeros((EXT, width), BF16)
    for g in range(groups):
        msg_ref[rows:, g * rows : (g + 1) * rows] = inner[g * EXT : (g + 1) * EXT].astype(BF16)
    msg_ref[rows:, (rank_groups - 1) * rows :] = two_parts(squares)


def squares_row(state):
    total = jnp.sum(state * state, axis=1, keepdims=True)
    rows = state.shape[0]
    return jnp.transpose(jnp.broadcast_to(total, (rows, rows)))[0:1, :]


def slot_masks(slots, first, count, shape):
    return [jnp.broadcast_to(slots[0:1, :] == float(j), shape) for j in range(first, first + count)]


def inner_partial(u, slots, down_refs, rank):
    first, total = 0, None
    rows = u.shape[0]
    for ref in down_refs:
        count = ref.shape[0] // rank
        product = dot(ref[...], u, CONTRACT_LAST)
        for j, mask in enumerate(slot_masks(slots, first, count, (rank, rows))):
            term = jnp.where(mask, product[j * rank : (j + 1) * rank], 0.0)
            total = term if total is None else total + term
        first += count
    return total


def first_kernel(even_ref, odd_ref, gain_ref, state_ref, slots_ref, msg_ref):
    cap = even_ref.shape[0]
    rows, width = state_ref.shape
    state_ref[:cap] = even_ref[:, :width]
    state_ref[cap:] = odd_ref[:, :width]
    lane = iota((8, rows), 1)
    even, odd = even_ref[:, width:].astype(F32)[0:8], odd_ref[:, width:].astype(F32)[0:8]
    slots_ref[...] = jnp.where(lane < cap, even, odd) - 1.0
    state = state_ref[...].astype(F32)
    msg_ref[:rows, :] = (state * gain_ref[...]).astype(BF16)
    put_extra(msg_ref, rows, None, squares_row(state))


def first_inner_kernel(msg0_ref, msg1_ref, slots0_ref, slots1_ref, own_ref, copy_ref, out_ref):
    rank, rows = out_ref.shape[0], out_ref.shape[1] // 2
    for h, (msg, slots) in enumerate(((msg0_ref, slots0_ref), (msg1_ref, slots1_ref))):
        out_ref[:, h * rows : (h + 1) * rows] = inner_partial(
            msg[:rows, :], slots[...], (own_ref, copy_ref), rank
        )


def block_kernel(n_blocks, at, last, place_ref, weight_ref, other_ref, *refs):
    msgs, refs = refs[:n_blocks], refs[n_blocks:]
    width = weight_ref.shape[1]
    rows = msgs[0].shape[0] - EXT
    if at[0] == 0:
        old = None
        outs = refs
    else:
        old, outs = refs[:3], refs[3:]
    mine = theirs = extra = None
    for i, msg in enumerate(msgs):
        q = place_ref[at[i]]
        u = msg[:rows, :]
        a = dot(u, weight_ref[pl.ds(pl.multiple_of((2 * q + place_ref[4]) * width, width), width), :])
        b = dot(u, other_ref[pl.ds(pl.multiple_of(q * width, width), width), :])
        e = msg[rows:, :].astype(F32)
        mine, theirs, extra = (a, b, e) if mine is None else (mine + a, theirs + b, extra + e)
    if old is not None:
        mine, theirs, extra = mine + old[0][...], theirs + old[1][...], extra + old[2][...]
    outs[0][...] = mine
    outs[2][...] = extra
    if not last:
        outs[1][...] = theirs
        return
    outs[1][:rows, :] = theirs.astype(BF16)
    outs[1][rows:, :] = extra.astype(BF16)
    tail = extra[:, width - rows :]
    outs[1][rows:, width - rows :] = two_parts(tail[0:1] + tail[1:2])


def finish_kernel(
    first, last, width_all, rank, mine_ref, extra_ref, got_ref, state_ref, slots_ref, gain_ref, down_ref, downc_ref, up_ref, upc_ref, *refs
):
    rows, width = state_ref.shape
    if first:
        inner_ref, refs = refs[0], refs[1:]
    extra = extra_ref[...] + got_ref[rows:, :].astype(F32)
    if first:
        inner = inner_ref[...]
    else:
        inner = jnp.concatenate(
            [extra[:, g * rows : (g + 1) * rows] for g in range(rank // EXT)], axis=0
        )
    tail = extra[:, width - rows :]
    scale = lax.rsqrt((tail[0:1] + tail[1:2]) / width_all + EPS)
    inner = (inner * scale).astype(BF16).astype(F32)
    slots = slots_ref[...]
    outer, begin = None, 0
    for ref in (up_ref, upc_ref):
        count = ref.shape[0] // rank
        spread = jnp.concatenate(
            [jnp.where(m, inner, 0.0) for m in slot_masks(slots, begin, count, (rank, rows))], axis=0
        ).astype(BF16)
        term = dot(spread, ref[...], CONTRACT_FIRST)
        outer = term if outer is None else outer + term
        begin += count
    delta = (adapter_scale * outer).astype(BF16).astype(F32)
    column = jnp.transpose(jnp.broadcast_to(scale, (rows, rows)))
    column = jnp.concatenate([column] * (width // rows), axis=1)
    base = (mine_ref[...] + got_ref[:rows, :].astype(F32)) * column
    state = (state_ref[...].astype(F32) + base + delta).astype(BF16)
    refs[0][...] = state
    if last:
        return
    msg_ref = refs[1]
    state = state.astype(F32)
    u = (state * gain_ref[...]).astype(BF16)
    msg_ref[:rows, :] = u
    put_extra(msg_ref, rows, inner_partial(u, slots, (down_ref, downc_ref), rank), squares_row(state))


def body(tokens, gain, base_projection_weight, adapter_down_weight, adapter_up_weight, plan, target, slot):
    groups = lax.axis_size("store")
    parts = lax.axis_size("mp")
    group = lax.axis_index("store")
    part = lax.axis_index("mp")
    n_tokens, width = tokens.shape
    owned, rank = adapter_down_weight.shape[:2]
    rows = 2 * CAP
    quarter = parts // 2
    place = part // 2
    core = part % 2

    def mp(x, pairs_of):
        return lax.ppermute(x, "mp", [(i, pairs_of(i)) for i in range(parts)])

    def sibling(x):
        return mp(x, lambda i: i ^ 1)

    def side_a(x):
        return mp(x, lambda i: i ^ (4 if i % 2 else 2))

    def side_b(x):
        return mp(x, lambda i: i ^ (2 if i % 2 else 4))

    def store(x, k):
        return lax.ppermute(x, "store", [(g, g ^ k) for g in range(groups)])

    perm, *chunks = call(
        sort_kernel,
        [((groups * CAP, n_tokens), BF16)] + [((CAP, width + rows), BF16)] * groups,
        [IN_SMEM] + [IN_VMEM] * 3,
        group.reshape(1).astype(jnp.int32),
        tokens,
        target.reshape(1, n_tokens),
        slot.reshape(1, n_tokens),
        name="sort",
    )
    chunks = [c if k == 0 else store(c, k) for k, c in enumerate(chunks)]

    blocks = base_projection_weight.reshape(quarter, 2, width, width)
    other = sibling(lax.dynamic_index_in_dim(blocks, 1 - core, 1, keepdims=False))
    other = other.reshape(quarter * width, width)

    down = adapter_down_weight.reshape(owned * rank, width)
    up = adapter_up_weight.reshape(owned * rank, width)
    down_copy, up_copy = fetch_copies(plan, [down, up], owned, group, groups)

    my_gain = lax.dynamic_slice_in_dim(gain, part * width, width, 0).reshape(1, width)
    near, far = jnp.where(core == 0, 1, 2), jnp.where(core == 0, 2, 1)
    places = jnp.stack([place, place ^ near, place ^ far, place ^ 3, core]).astype(jnp.int32)

    halves = range(groups // 2)
    state, slots, msg = [], [], []
    for h in halves:
        s, l, m = call(
            first_kernel,
            [((rows, width), BF16), ((8, rows), F32), ((rows + EXT, width), BF16)],
            [IN_VMEM] * 3,
            chunks[2 * h],
            chunks[2 * h + 1],
            my_gain,
            name="first",
        )
        state.append(s)
        slots.append(l)
        msg.append(m)
    inner = call(
        first_inner_kernel,
        ((rank, 2 * rows), F32),
        [IN_VMEM] * 6,
        msg[0],
        msg[1],
        slots[0],
        slots[1],
        down,
        down_copy,
        name="first_inner",
    )
    for k in (2, 4, 1):
        inner = inner + mp(inner, lambda i: i ^ k)

    acc = ((rows, width), F32)
    ext = ((EXT, width), F32)
    message = ((rows + EXT, width), BF16)
    work = 4 * rows * width * width

    def blocks_of(msgs, at, old, last):
        return call(
            functools.partial(block_kernel, len(msgs), at, last),
            [acc, message if last else acc, ext],
            [IN_SMEM] + [IN_VMEM] * (2 + len(msgs) + len(old)),
            places,
            base_projection_weight,
            other,
            *msgs,
            *old,
            flops=work * len(msgs),
            name="blocks",
        )

    for step in range(STEPS):
        final = step == STEPS - 1
        for h in halves:
            a = side_a(msg[h])
            b = side_b(msg[h])
            old = blocks_of([msg[h]], (0,), (), False)
            d = side_b(a)
            old = blocks_of([a, b], (1, 2), old, False)
            mine, theirs, extra = blocks_of([d], (3,), old, True)
            got = sibling(theirs)
            args = [mine, extra, got, state[h], slots[h], my_gain, down, down_copy, up, up_copy]
            if step == 0:
                args.append(inner[:, h * rows : (h + 1) * rows])
            outs = call(
                functools.partial(finish_kernel, step == 0, final, parts * width, rank),
                [((rows, width), BF16)] + ([] if final else [message]),
                [IN_VMEM] * len(args),
                *args,
                flops=work,
                name="finish",
            )
            state[h] = outs[0]
            if not final:
                msg[h] = outs[1]

    back = []
    for h in halves:
        for j in range(2):
            k = 2 * h + j
            chunk = state[h][j * CAP : (j + 1) * CAP]
            back.append(chunk if k == 0 else store(chunk, k))
    return call(
        unsort_kernel,
        ((n_tokens, width), BF16),
        [IN_VMEM] * (1 + groups),
        perm,
        *back,
        name="unsort",
    )


def plain_body(
    tokens, gain, base_projection_weight, adapter_down_weight, adapter_up_weight, plan, target, slot
):
    store_count = lax.axis_size("store")
    group = lax.axis_index("store")
    owned_adapters, rank, width = adapter_down_weight.shape
    replica_count = plan.shape[1]
    n_slots = owned_adapters + replica_count
    owner = plan // owned_adapters
    local = plan % owned_adapters
    select = jnp.logical_and(
        (owner == group)[:, :, None],
        local[:, :, None] == jnp.arange(owned_adapters, dtype=jnp.int32)[None, None, :],
    )
    select = select.astype(BF16).reshape(store_count * replica_count, owned_adapters)

    def held(own):
        send = jnp.dot(select, own.reshape(owned_adapters, rank * width), preferred_element_type=F32)
        send = send.astype(BF16).reshape(store_count, replica_count, rank * width)
        got = lax.all_to_all(send, "store", split_axis=0, concat_axis=0, tiled=True)
        got = jnp.sum(got.astype(F32), axis=0).astype(BF16)
        both = jnp.concatenate([own, got.reshape(replica_count, rank, width)], 0)
        return both.reshape(n_slots * rank, width)

    host_down, host_up = held(adapter_down_weight), held(adapter_up_weight)
    target_group = target[:, 0]
    n_tokens = target_group.shape[0]
    member = (target_group[:, None] == jnp.arange(store_count, dtype=jnp.int32)[None, :]).astype(BF16)
    order = jnp.arange(n_tokens)
    before = (order[:, None] > order[None, :]).astype(BF16)
    earlier = jnp.dot(before, member, preferred_element_type=F32)
    place = jnp.sum(earlier * member.astype(F32), axis=1).astype(jnp.int32)
    row_index = target_group * CAP + place
    slots = jnp.full((store_count * CAP,), -1, jnp.int32).at[row_index].set(slot)
    state = jnp.zeros((store_count * CAP, width), BF16).at[row_index].set(tokens)

    def exchange(x):
        return lax.all_to_all(
            x.reshape(store_count, CAP, -1), "store", split_axis=0, concat_axis=0, tiled=True
        ).reshape(store_count * CAP, -1)

    state = exchange(state)
    selected = exchange(slots) == jnp.arange(n_slots, dtype=jnp.int32)[None, :]
    total_rows = state.shape[0]
    column_start = lax.axis_index("mp") * width
    for step in range(STEPS):
        whole = lax.all_gather(state, "mp", axis=1, tiled=True)
        values = whole.astype(F32)
        mean_sq = jnp.mean(values * values, axis=1, keepdims=True)
        normed = (values * lax.rsqrt(mean_sq + EPS) * gain[None, :]).astype(BF16)
        mine = lax.dynamic_slice_in_dim(normed, column_start, width, 1)
        partial_value = lax.dot_general(mine, host_down, CONTRACT_LAST, preferred_element_type=F32)
        partial_value = jnp.sum(
            partial_value.reshape(total_rows, n_slots, rank) * selected[:, :, None].astype(F32), axis=1
        )
        inner = lax.psum(partial_value, "mp").astype(BF16)
        spread = (selected[:, :, None].astype(BF16) * inner[:, None, :]).reshape(total_rows, -1)
        outer = jnp.dot(spread, host_up, preferred_element_type=F32)
        delta = (adapter_scale * outer).astype(BF16).astype(F32)
        base = jnp.dot(normed, base_projection_weight, preferred_element_type=F32)
        state = (state.astype(F32) + base + delta).astype(BF16)
    return exchange(state)[row_index]


def solution(mesh):
    parts, groups = mesh.shape["mp"], mesh.shape["store"]

    def run(tokens, *rest):
        width = tokens.shape[1] // parts
        rank = rest[2].shape[1]
        rows = 2 * CAP
        cube = parts == 8 and groups == 4
        fits = rank % EXT == 0 and width % rows == 0 and rank // EXT + 1 <= width // rows
        return jax.shard_map(
            body if cube and fits else plain_body,
            mesh=mesh,
            in_specs=(
                P("store", "mp"),
                P(),
                P(None, "mp"),
                P("store", None, "mp"),
                P("store", None, "mp"),
                P(),
                P("store", None),
                P("store"),
            ),
            out_specs=P("store", "mp"),
            check_vma=False,
        )(tokens, *rest)

    return run
```

```python
import functools
import math

import jax
import jax.numpy as jnp
from jax import lax
from jax.experimental import pallas as pl
from jax.experimental.pallas import tpu as pltpu
from jax.sharding import PartitionSpec as P

STEPS = 4
CAP = 64
EPS = 1e-05
EXT = 16
MIB = 2**20

adapter_scale = 0.5

F32 = jnp.float32
BF16 = jnp.bfloat16
IN_VMEM = pl.BlockSpec(memory_space=pltpu.VMEM)
IN_SMEM = pl.BlockSpec(memory_space=pltpu.SMEM)
CONTRACT_LAST = (((1,), (1,)), ((), ()))
CONTRACT_FIRST = (((0,), (0,)), ((), ()))


def pinned(x):
    return pltpu.with_memory_space_constraint(x, pltpu.VMEM)


def call(kernel, out, specs, *args, name=None, scratch=(), pin=False, after=()):
    many = isinstance(out, list)
    n_args, kernel_of = len(args), kernel
    if after:
        args, specs = (*args, *after), [*specs] + [pl.BlockSpec(memory_space=pl.ANY)] * len(after)

        def kernel(*refs):
            kernel_of(*refs[:n_args], *refs[n_args + len(after) :])

    kind = pltpu.VMEM if pin else jax.ShapeDtypeStruct
    shapes = [kind(s, d) for s, d in (out if many else [out])]
    r = pl.pallas_call(
        kernel,
        out_shape=shapes,
        in_specs=specs,
        out_specs=[IN_VMEM] * len(shapes),
        scratch_shapes=scratch,
        compiler_params=pltpu.CompilerParams(vmem_limit_bytes=12 * MIB),
        cost_estimate=pl.CostEstimate(flops=0, bytes_accessed=0, transcendentals=0),
        name=name,
    )(*args)
    return r if many else r[0]


def dot(a, b, dims=(((1,), (0,)), ((), ()))):
    return lax.dot_general(a, b, dims, preferred_element_type=F32)


def iota(shape, dim):
    return lax.broadcasted_iota(jnp.int32, shape, dim)


def sort_kernel(tokens_ref, target_ref, slot_ref, perm_ref, *chunk_refs):
    n_tokens, width = tokens_ref.shape
    groups = len(chunk_refs)
    rows = groups * CAP
    apart = jnp.bitwise_xor(target_ref[...], lax.axis_index("store"))
    member = (iota((max(8, groups), n_tokens), 0) == apart).astype(F32)
    before = (iota((n_tokens, n_tokens), 0) < iota((n_tokens, n_tokens), 1)).astype(BF16)
    earlier = dot(member.astype(BF16), before)
    place = jnp.sum(earlier * member, axis=0, keepdims=True).astype(jnp.int32)
    perm = (iota((rows, n_tokens), 0) == apart * CAP + place).astype(F32).astype(BF16)
    perm_ref[...] = perm
    sorted_rows = dot(perm, tokens_ref[...]).astype(BF16)
    slots = jnp.broadcast_to((slot_ref[...] + 1).astype(F32), (8, n_tokens)).astype(BF16)
    slots = dot(slots, perm, CONTRACT_LAST)
    lanes = 2 * CAP
    for k, ref in enumerate(chunk_refs):
        ref[:, :width] = sorted_rows[k * CAP : (k + 1) * CAP]
        half = slots[:, (k // 2) * lanes : (k // 2 + 1) * lanes]
        ref[:, width:] = jnp.concatenate([half, jnp.zeros((CAP - 8, lanes), F32)], 0).astype(BF16)


def unsort_kernel(perm_ref, *refs):
    rows = jnp.concatenate([r[...] for r in refs[:-1]], axis=0)
    refs[-1][...] = dot(perm_ref[...], rows, CONTRACT_FIRST).astype(BF16)


def order_of(plan_ref, owned, end, far):
    asked = []
    for l in range(owned):
        hit = [plan_ref[far, i] == end * owned + l for i in range(plan_ref.shape[1])]
        asked.append(functools.reduce(jnp.logical_or, hit).astype(jnp.int32))
    total, seen, places = sum(asked), 0, []
    for l in range(owned):
        places.append(jnp.where(asked[l] == 1, seen, total + l - seen))
        seen = seen + asked[l]
    return places


def chosen(values, index):
    out = values[0]
    for i in range(1, len(values)):
        out = jnp.where(index == i, values[i], out)
    return out


def end_blocks(owned, plan_ref, own_ref, out_refs):
    copies = plan_ref.shape[1]
    rank = own_ref.shape[0] // owned
    group = lax.axis_index("store")
    end = jnp.where(group < 2, 0, 3)
    for l, place in enumerate(order_of(plan_ref, owned, end, 3 - end)):
        for block, out_ref in enumerate(out_refs):

            @pl.when(jnp.logical_and(place // copies == block, group == end))
            def _():
                at = pl.multiple_of((place % copies) * rank, rank)
                out_ref[pl.ds(at, rank), :] = own_ref[l * rank : (l + 1) * rank, :]

    for i in range(copies):

        @pl.when(group != end)
        def _():
            at = pl.multiple_of((plan_ref[end, i] % owned) * rank, rank)
            out_refs[0][i * rank : (i + 1) * rank, :] = own_ref[pl.ds(at, rank), :]


def end_blocks_kernel(owned, plan_ref, own_ref, low_ref, high_ref):
    end_blocks(owned, plan_ref, own_ref, (low_ref, high_ref))


def front_kernel(owned, plan_ref, own_ref, tokens_ref, target_ref, slot_ref, low_ref, high_ref, *refs):
    end_blocks(owned, plan_ref, own_ref, (low_ref, high_ref))
    sort_kernel(tokens_ref, target_ref, slot_ref, *refs)


def pass_kernel(owned, dest_of, n_blocks, plan_ref, own_ref, *refs):
    out_ref = refs[-1]
    copies = plan_ref.shape[1]
    rank = own_ref.shape[0] // owned
    group = lax.axis_index("store")
    end = jnp.where(group < 2, 0, 3)
    places = order_of(plan_ref, owned, end, 3 - end)
    for i in range(copies):
        adapter = plan_ref[chosen(dest_of, group), i]
        owner, local = adapter // owned, adapter % owned
        at = slice(i * rank, (i + 1) * rank)

        @pl.when(owner == group)
        def _():
            out_ref[at, :] = own_ref[pl.ds(pl.multiple_of(local * rank, rank), rank), :]

        place = chosen(places, local)
        begin = pl.multiple_of((place % copies) * rank, rank)
        for j in range(n_blocks):

            @pl.when(jnp.logical_and(owner != group, place // copies == j))
            def _():
                out_ref[at, :] = refs[j][pl.ds(begin, rank), :]

        if n_blocks == 1:

            @pl.when(jnp.logical_and(owner != group, place // copies > 0))
            def _():
                out_ref[at, :] = refs[0][at, :]


def gather_kernel(owned, plan_ref, low_ref, high_ref, passed_ref, far_ref, out_ref):
    copies = plan_ref.shape[1]
    rank = out_ref.shape[0] // copies
    group = lax.axis_index("store")
    end = jnp.where(group < 2, 0, 3)
    beside = jnp.where(group < 2, 1, 2)
    places = order_of(plan_ref, owned, end, 3 - end)
    for i in range(copies):
        adapter = plan_ref[group, i]
        owner, local = adapter // owned, adapter % owned
        at = slice(i * rank, (i + 1) * rank)
        place = chosen(places, local)
        begin = pl.multiple_of((place % copies) * rank, rank)
        middle = group == beside

        def put(condition, value_of):
            @pl.when(condition)
            def _():
                out_ref[at, :] = value_of()

        raw = jnp.logical_and(middle, owner == end)
        put(jnp.logical_and(raw, place < copies), lambda: low_ref[pl.ds(begin, rank), :])
        put(jnp.logical_and(raw, place >= copies), lambda: high_ref[pl.ds(begin, rank), :])
        put(jnp.logical_and(middle, owner != end), lambda: passed_ref[at, :])
        put(jnp.logical_and(group == end, owner == beside), lambda: low_ref[at, :])
        put(jnp.logical_and(group == end, owner != beside), lambda: far_ref[at, :])


def fetch_copies(plan, own, owned, front):
    copies = plan.shape[1]
    rank = own[0].shape[0] // owned
    shape = ((copies * rank, own[0].shape[1]), BF16)

    def make(kernel, *args, out=shape, after=()):
        return call(kernel, out, [IN_SMEM] + [IN_VMEM] * len(args), plan, *args, name="pick", after=after)

    def send(x, pairs):
        return lax.ppermute(x, "store", pairs)

    def passing(dest_of, i, *blocks, after=()):
        return make(functools.partial(pass_kernel, owned, dest_of, len(blocks)), own[i], *blocks, after=after)

    pairs, ends, middle, across = [(0, 1), (1, 0), (2, 3), (3, 2)], [(0, 1), (3, 2)], [(1, 2), (2, 1)], [(1, 3), (2, 0)]
    low, high, got = {}, {}, []
    (low[0], high[0]), chunks, rest = front(shape)
    low[0], high[0] = send(low[0], pairs), send(high[0], ends)
    low[1], high[1] = make(
        functools.partial(end_blocks_kernel, owned), own[1], out=[shape, shape], after=[low[0], *chunks[1:]]
    )
    low[1], high[1] = send(low[1], pairs), send(high[1], ends)
    for i in range(2):
        far = send(passing((3, 3, 0, 0), i, low[i]), across)
        passed = send(passing((2, 2, 1, 1), i, low[i], high[i]), middle)
        got.append(make(functools.partial(gather_kernel, owned), low[i], high[i], passed, far))
    return got, chunks, rest, low[0]


def apart_kernel(weight_ref, sent_ref, sems):
    width = weight_ref.shape[1]
    other = 1 - lax.axis_index("mp") % 2
    copies = []
    for q in range(sent_ref.shape[0] // width):
        start = pl.multiple_of((2 * q + other) * width, width)
        copies.append(
            pltpu.make_async_copy(
                weight_ref.at[pl.ds(start, width), :], sent_ref.at[pl.ds(q * width, width), :], sems.at[q]
            )
        )
    for copy in copies:
        copy.start()
    for copy in copies:
        copy.wait()


def two_parts(row):
    high = row.astype(BF16).astype(F32)
    at = iota((EXT, row.shape[1]), 0)
    return jnp.where(at == 0, high, jnp.where(at == 1, row - high, 0.0)).astype(BF16)


def put_extra(msg_ref, rows, inner, squares):
    width = msg_ref.shape[1]
    groups = 0 if inner is None else inner.shape[0] // EXT
    rank_groups = width // rows
    msg_ref[rows:, :] = jnp.zeros((EXT, width), BF16)
    for g in range(groups):
        msg_ref[rows:, g * rows : (g + 1) * rows] = inner[g * EXT : (g + 1) * EXT].astype(BF16)
    msg_ref[rows:, (rank_groups - 1) * rows :] = two_parts(squares)


def squares_row(state):
    total = jnp.sum(state * state, axis=1, keepdims=True)
    rows = state.shape[0]
    return jnp.transpose(jnp.broadcast_to(total, (rows, rows)))[0:1, :]


def slot_masks(slots, first, count, shape):
    return [jnp.broadcast_to(slots[0:1, :] == float(j), shape) for j in range(first, first + count)]


def inner_partial(u, slots, down_refs, rank):
    first, total = 0, None
    rows = u.shape[0]
    for ref in down_refs:
        count = ref.shape[0] // rank
        product = dot(ref[...], u, CONTRACT_LAST)
        for j, mask in enumerate(slot_masks(slots, first, count, (rank, rows))):
            term = jnp.where(mask, product[j * rank : (j + 1) * rank], 0.0)
            total = term if total is None else total + term
        first += count
    return total


def my_columns(gain_ref, width):
    return gain_ref[:, pl.ds(pl.multiple_of(lax.axis_index("mp") * width, width), width)]


def first_kernel(gain_ref, *refs):
    n = (len(refs) - 1) // 4
    chunk_refs, state_refs, slots_refs, msg_ref = refs[: 2 * n], refs[2 * n : 3 * n], refs[3 * n : 4 * n], refs[4 * n]
    for h in range(n):
        even_ref, odd_ref, state_ref, slots_ref = chunk_refs[2 * h], chunk_refs[2 * h + 1], state_refs[h], slots_refs[h]
        cap = even_ref.shape[0]
        rows, width = state_ref.shape
        state_ref[:cap] = even_ref[:, :width]
        state_ref[cap:] = odd_ref[:, :width]
        lane = iota((8, rows), 1)
        even, odd = even_ref[:, width:].astype(F32)[0:8], odd_ref[:, width:].astype(F32)[0:8]
        slots_ref[...] = jnp.where(lane < cap, even, odd) - 1.0
        state = state_ref[...].astype(F32)
        part_ref = msg_ref.at[h * (rows + EXT) : (h + 1) * (rows + EXT)]
        part_ref[:rows, :] = (state * my_columns(gain_ref, width)).astype(BF16)
        put_extra(part_ref, rows, None, squares_row(state))


def first_inner_kernel(msg_ref, slots0_ref, slots1_ref, own_ref, copy_ref, out_ref):
    rank, rows = out_ref.shape[0], out_ref.shape[1] // 2
    for h, slots in enumerate((slots0_ref, slots1_ref)):
        u = msg_ref[h * (rows + EXT) : h * (rows + EXT) + rows, :]
        out_ref[:, h * rows : (h + 1) * rows] = inner_partial(u, slots[...], (own_ref, copy_ref), rank)


def block_kernel(n_blocks, n_halves, at, last, weight_ref, other_ref, *refs):
    msgs, refs = refs[:n_blocks], refs[n_blocks:]
    width = weight_ref.shape[1]
    rows = msgs[0].shape[0] // n_halves - EXT
    if at[0] == 0:
        old = None
        outs = refs
    else:
        old, outs = refs[:3], refs[3:]
    mine = theirs = extra = None
    part = lax.axis_index("mp")
    core = part % 2

    def both(msg, under):
        parts = []
        for h in range(n_halves):
            begin = h * (rows + EXT)
            parts.append(msg[begin + rows : begin + rows + EXT, :] if under else msg[begin : begin + rows, :])
        return parts[0] if n_halves == 1 else jnp.concatenate(parts, axis=0)

    for i, msg in enumerate(msgs):
        q = jnp.bitwise_xor(part // 2, (0, 1 + core, 2 - core, 3)[at[i]])
        u = both(msg, False)
        a = dot(u, weight_ref[pl.ds(pl.multiple_of((2 * q + core) * width, width), width), :])
        b = dot(u, other_ref[pl.ds(pl.multiple_of(q * width, width), width), :])
        e = both(msg, True).astype(F32)
        mine, theirs, extra = (a, b, e) if mine is None else (mine + a, theirs + b, extra + e)
    if old is not None:
        mine, theirs, extra = mine + old[0][...], theirs + old[1][...], extra + old[2][...]
    outs[0][...] = mine
    outs[2][...] = extra
    if not last:
        outs[1][...] = theirs
        return
    for h in range(n_halves):
        begin = h * (rows + EXT)
        outs[1][begin : begin + rows, :] = theirs[h * rows : (h + 1) * rows].astype(BF16)
        under = extra[h * EXT : (h + 1) * EXT]
        outs[1][begin + rows : begin + rows + EXT, :] = under.astype(BF16)
        tail = under[:, width - rows :]
        outs[1][begin + rows : begin + rows + EXT, width - rows :] = two_parts(tail[0:1] + tail[1:2])


def finish_kernel(
    n_halves, h, last, rank, mine_ref, extra_ref, got_ref, state_ref, slots_ref, gain_ref, down_ref, downc_ref, up_ref, upc_ref, *refs
):
    rows, width = state_ref.shape
    width_all = gain_ref.shape[1]
    if n_halves > 1:
        inner_ref, refs = refs[0], refs[1:]
    begin = h * (rows + EXT)
    extra = extra_ref[h * EXT : (h + 1) * EXT, :] + got_ref[begin + rows : begin + rows + EXT, :].astype(F32)
    if n_halves > 1:
        inner = inner_ref[:, h * rows : (h + 1) * rows]
    else:
        inner = jnp.concatenate(
            [extra[:, g * rows : (g + 1) * rows] for g in range(rank // EXT)], axis=0
        )
    tail = extra[:, width - rows :]
    scale = lax.rsqrt((tail[0:1] + tail[1:2]) / width_all + EPS)
    inner = (inner * scale).astype(BF16).astype(F32)
    slots = slots_ref[...]
    outer, held = None, 0
    for ref in (up_ref, upc_ref):
        count = ref.shape[0] // rank
        spread = jnp.concatenate(
            [jnp.where(m, inner, 0.0) for m in slot_masks(slots, held, count, (rank, rows))], axis=0
        ).astype(BF16)
        term = dot(spread, ref[...], CONTRACT_FIRST)
        outer = term if outer is None else outer + term
        held += count
    delta = (adapter_scale * outer).astype(BF16).astype(F32)
    column = jnp.transpose(jnp.broadcast_to(scale, (rows, rows)))
    column = jnp.concatenate([column] * (width // rows), axis=1)
    base = (mine_ref[h * rows : (h + 1) * rows, :] + got_ref[begin : begin + rows, :].astype(F32)) * column
    state = (state_ref[...].astype(F32) + base + delta).astype(BF16)
    if last:
        refs[0][...] = state[: rows // 2]
        refs[1][...] = state[rows // 2 :]
        return
    refs[0][...] = state
    msg_ref = refs[1]
    state = state.astype(F32)
    u = (state * my_columns(gain_ref, width)).astype(BF16)
    msg_ref[:rows, :] = u
    put_extra(msg_ref, rows, inner_partial(u, slots, (down_ref, downc_ref), rank), squares_row(state))


def body(tokens, gain, base_projection_weight, adapter_down_weight, adapter_up_weight, plan, target, slot):
    groups = lax.axis_size("store")
    parts = lax.axis_size("mp")
    n_tokens, width = tokens.shape
    owned, rank = adapter_down_weight.shape[:2]
    rows = 2 * CAP
    gain = gain.reshape(1, parts * width)

    def mp(x, pairs_of):
        return lax.ppermute(x, "mp", [(i, pairs_of(i)) for i in range(parts)])

    def sibling(x):
        return mp(x, lambda i: i ^ 1)

    def side_a(x):
        return mp(x, lambda i: i ^ (4 if i % 2 else 2))

    def side_b(x):
        return mp(x, lambda i: i ^ (2 if i % 2 else 4))

    def store(x, k):
        return lax.ppermute(x, "store", [(g, g ^ k) for g in range(groups)])

    down = adapter_down_weight.reshape(owned * rank, width)
    up = adapter_up_weight.reshape(owned * rank, width)

    def front(shape):
        low, high, perm, *chunks = call(
            functools.partial(front_kernel, owned),
            [shape, shape, ((groups * CAP, n_tokens), BF16)] + [((CAP, width + rows), BF16)] * groups,
            [IN_SMEM] + [IN_VMEM] * 4,
            plan,
            *(
                pltpu.with_memory_space_constraint(x, pltpu.HBM)
                for x in (down, tokens, target.reshape(1, n_tokens), slot.reshape(1, n_tokens))
            ),
            name="front",
        )
        return (low, high), [c if k == 0 else store(c, k) for k, c in enumerate(chunks)], perm

    (down_copy, up_copy), chunks, perm, early = fetch_copies(plan, [down, up], owned, front)

    other = call(
        apart_kernel,
        ((parts // 2 * width, width), BF16),
        [pl.BlockSpec(memory_space=pl.ANY)],
        pltpu.with_memory_space_constraint(base_projection_weight, pltpu.HBM),
        name="apart",
        scratch=[pltpu.SemaphoreType.DMA((parts // 2,))],
        after=[perm],
    )
    weight, other = pinned(base_projection_weight), pinned(sibling(other))

    halves = range(groups // 2)
    n = len(halves)
    acc = ((rows, width), F32)
    message = ((rows + EXT, width), BF16)

    def blocks_of(n_halves, msgs, at, old, last):
        many = [((n_halves * r, c), d) for (r, c), d in (acc, message if last else acc, ((EXT, width), F32))]
        return call(
            functools.partial(block_kernel, len(msgs), n_halves, at, last),
            many,
            [IN_VMEM] * (2 + len(msgs) + len(old)),
            weight,
            other,
            *msgs,
            *old,
            name="blocks",
        )

    def exchange(n_halves, msg):
        a = side_a(msg)
        b = side_b(msg)
        old = blocks_of(n_halves, [msg], (0,), (), False)
        d = side_b(a)
        old = blocks_of(n_halves, [a, b], (1, 2), old, False)
        mine, theirs, extra = blocks_of(n_halves, [d], (3,), old, True)
        return mine, extra, sibling(theirs)

    def finish(n_halves, h, final, sums, state, slots, inner=()):
        args = [*sums, state, slots, gain, down, down_copy, up, up_copy, *inner]
        return call(
            functools.partial(finish_kernel, n_halves, h, final, rank),
            [((CAP, width), BF16)] * 2 if final else [((rows, width), BF16), message],
            [IN_VMEM] * len(args),
            *args,
            name="finish",
        )

    outs = call(
        first_kernel,
        [((rows, width), BF16)] * n + [((8, rows), F32)] * n + [((n * (rows + EXT), width), BF16)],
        [IN_VMEM] * (1 + groups),
        gain,
        *chunks,
        name="first",
        after=[early, other],
    )
    state, slots, msg = outs[:n], outs[n : 2 * n], outs[-1]
    sums = exchange(n, msg)
    inner = call(
        first_inner_kernel, ((rank, n * rows), F32), [IN_VMEM] * 5, msg, *slots, down, down_copy, name="first_inner"
    )
    for k in (2, 4, 1):
        inner = inner + mp(inner, lambda i: i ^ k)
    outs = [finish(n, h, False, sums, state[h], slots[h], [inner]) for h in halves]
    state, msg = [o[0] for o in outs], [o[1] for o in outs]
    for step in range(1, STEPS):
        final = step == STEPS - 1
        for h in halves:
            outs = finish(1, 0, final, exchange(1, msg[h]), state[h], slots[h])
            if final:
                state[h] = outs
            else:
                state[h], msg[h] = outs

    back = [c if k == 0 else store(c, k) for k, c in enumerate(sum(map(list, state), []))]
    return call(
        unsort_kernel,
        ((n_tokens, width), BF16),
        [IN_VMEM] * (1 + groups),
        perm,
        *back,
        name="unsort",
    )


def plain_body(
    tokens, gain, base_projection_weight, adapter_down_weight, adapter_up_weight, plan, target, slot
):
    store_count = lax.axis_size("store")
    group = lax.axis_index("store")
    owned_adapters, rank, width = adapter_down_weight.shape
    replica_count = plan.shape[1]
    n_slots = owned_adapters + replica_count
    owner = plan // owned_adapters
    local = plan % owned_adapters
    select = jnp.logical_and(
        (owner == group)[:, :, None],
        local[:, :, None] == jnp.arange(owned_adapters, dtype=jnp.int32)[None, None, :],
    )
    select = select.astype(BF16).reshape(store_count * replica_count, owned_adapters)

    def held(own):
        send = jnp.dot(select, own.reshape(owned_adapters, rank * width), preferred_element_type=F32)
        send = send.astype(BF16).reshape(store_count, replica_count, rank * width)
        got = lax.all_to_all(send, "store", split_axis=0, concat_axis=0, tiled=True)
        got = jnp.sum(got.astype(F32), axis=0).astype(BF16)
        both = jnp.concatenate([own, got.reshape(replica_count, rank, width)], 0)
        return both.reshape(n_slots * rank, width)

    host_down, host_up = held(adapter_down_weight), held(adapter_up_weight)
    target_group = target[:, 0]
    n_tokens = target_group.shape[0]
    member = (target_group[:, None] == jnp.arange(store_count, dtype=jnp.int32)[None, :]).astype(BF16)
    order = jnp.arange(n_tokens)
    before = (order[:, None] > order[None, :]).astype(BF16)
    earlier = jnp.dot(before, member, preferred_element_type=F32)
    place = jnp.sum(earlier * member.astype(F32), axis=1).astype(jnp.int32)
    row_index = target_group * CAP + place
    slots = jnp.full((store_count * CAP,), -1, jnp.int32).at[row_index].set(slot)
    state = jnp.zeros((store_count * CAP, width), BF16).at[row_index].set(tokens)

    def exchange(x):
        return lax.all_to_all(
            x.reshape(store_count, CAP, -1), "store", split_axis=0, concat_axis=0, tiled=True
        ).reshape(store_count * CAP, -1)

    state = exchange(state)
    selected = exchange(slots) == jnp.arange(n_slots, dtype=jnp.int32)[None, :]
    total_rows = state.shape[0]
    column_start = lax.axis_index("mp") * width
    for step in range(STEPS):
        whole = lax.all_gather(state, "mp", axis=1, tiled=True)
        values = whole.astype(F32)
        mean_sq = jnp.mean(values * values, axis=1, keepdims=True)
        normed = (values * lax.rsqrt(mean_sq + EPS) * gain[None, :]).astype(BF16)
        mine = lax.dynamic_slice_in_dim(normed, column_start, width, 1)
        partial_value = lax.dot_general(mine, host_down, CONTRACT_LAST, preferred_element_type=F32)
        partial_value = jnp.sum(
            partial_value.reshape(total_rows, n_slots, rank) * selected[:, :, None].astype(F32), axis=1
        )
        inner = lax.psum(partial_value, "mp").astype(BF16)
        spread = (selected[:, :, None].astype(BF16) * inner[:, None, :]).reshape(total_rows, -1)
        outer = jnp.dot(spread, host_up, preferred_element_type=F32)
        delta = (adapter_scale * outer).astype(BF16).astype(F32)
        base = jnp.dot(normed, base_projection_weight, preferred_element_type=F32)
        state = (state.astype(F32) + base + delta).astype(BF16)
    return exchange(state)[row_index]


def solution(mesh):
    parts, groups = mesh.shape["mp"], mesh.shape["store"]

    def run(tokens, *rest):
        width = tokens.shape[1] // parts
        rank = rest[2].shape[1]
        rows = 2 * CAP
        cube = parts == 8 and groups == 4
        cube = cube and rest[2].shape[0] == 2 * groups * rest[4].shape[1]
        fits = rank % EXT == 0 and width % rows == 0 and rank // EXT + 1 <= width // rows
        return jax.shard_map(
            body if cube and fits else plain_body,
            mesh=mesh,
            in_specs=(
                P("store", "mp"),
                P(),
                P(None, "mp"),
                P("store", None, "mp"),
                P("store", None, "mp"),
                P(),
                P("store", None),
                P("store"),
            ),
            out_specs=P("store", "mp"),
            check_vma=False,
        )(tokens, *rest)

    return run
```

```python
import functools
import math

import jax
import jax.numpy as jnp
from jax import lax
from jax.experimental import pallas as pl
from jax.experimental.pallas import tpu as pltpu
from jax.sharding import PartitionSpec as P

STEPS = 4
CAP = 64
EPS = 1e-05
EXT = 16
MIB = 2**20

adapter_scale = 0.5
ORDER_US = {'near1': 5, 'far1': 5, 'ends1': 10, 'first': 20}

F32 = jnp.float32
BF16 = jnp.bfloat16
IN_VMEM = pl.BlockSpec(memory_space=pltpu.VMEM)
IN_SMEM = pl.BlockSpec(memory_space=pltpu.SMEM)
CONTRACT_LAST = (((1,), (1,)), ((), ()))
CONTRACT_FIRST = (((0,), (0,)), ((), ()))


def pinned(x):
    return pltpu.with_memory_space_constraint(x, pltpu.VMEM)


def call(kernel, out, specs, *args, name=None, scratch=(), pin=False, after=()):
    many = isinstance(out, list)
    n_args, kernel_of = len(args), kernel
    if after:
        args, specs = (*args, *after), [*specs] + [pl.BlockSpec(memory_space=pl.ANY)] * len(after)

        def kernel(*refs):
            kernel_of(*refs[:n_args], *refs[n_args + len(after) :])

    kind = pltpu.VMEM if pin else jax.ShapeDtypeStruct
    shapes = [kind(s, d) for s, d in (out if many else [out])]
    r = pl.pallas_call(
        kernel,
        out_shape=shapes,
        in_specs=specs,
        out_specs=[IN_VMEM] * len(shapes),
        scratch_shapes=scratch,
        compiler_params=pltpu.CompilerParams(vmem_limit_bytes=12 * MIB),
        cost_estimate=pl.CostEstimate(flops=int(ORDER_US.get(name, 0) * 1.15e9), bytes_accessed=0, transcendentals=0),
        name=name,
    )(*args)
    return r if many else r[0]


def dot(a, b, dims=(((1,), (0,)), ((), ()))):
    return lax.dot_general(a, b, dims, preferred_element_type=F32)


def iota(shape, dim):
    return lax.broadcasted_iota(jnp.int32, shape, dim)


def sort_kernel(tokens_ref, target_ref, slot_ref, perm_ref, *chunk_refs):
    n_tokens, width = tokens_ref.shape
    groups = len(chunk_refs)
    rows = groups * CAP
    apart = jnp.bitwise_xor(target_ref[...], lax.axis_index("store"))
    member = (iota((max(8, groups), n_tokens), 0) == apart).astype(F32)
    before = (iota((n_tokens, n_tokens), 0) < iota((n_tokens, n_tokens), 1)).astype(BF16)
    earlier = dot(member.astype(BF16), before)
    place = jnp.sum(earlier * member, axis=0, keepdims=True).astype(jnp.int32)
    perm = (iota((rows, n_tokens), 0) == apart * CAP + place).astype(F32).astype(BF16)
    perm_ref[...] = perm
    sorted_rows = dot(perm, tokens_ref[...]).astype(BF16)
    slots = jnp.broadcast_to((slot_ref[...] + 1).astype(F32), (8, n_tokens)).astype(BF16)
    slots = dot(slots, perm, CONTRACT_LAST)
    lanes = 2 * CAP
    for k, ref in enumerate(chunk_refs):
        ref[:, :width] = sorted_rows[k * CAP : (k + 1) * CAP]
        half = slots[:, (k // 2) * lanes : (k // 2 + 1) * lanes]
        ref[:, width:] = jnp.concatenate([half, jnp.zeros((CAP - 8, lanes), F32)], 0).astype(BF16)


def unsort_kernel(perm_ref, *refs):
    rows = jnp.concatenate([r[...] for r in refs[:-1]], axis=0)
    refs[-1][...] = dot(perm_ref[...], rows, CONTRACT_FIRST).astype(BF16)


def order_of(plan_ref, owned, end, far):
    asked = []
    for l in range(owned):
        hit = [plan_ref[far, i] == end * owned + l for i in range(plan_ref.shape[1])]
        asked.append(functools.reduce(jnp.logical_or, hit).astype(jnp.int32))
    total, seen, places = sum(asked), 0, []
    for l in range(owned):
        places.append(jnp.where(asked[l] == 1, seen, total + l - seen))
        seen = seen + asked[l]
    return places


def chosen(values, index):
    out = values[0]
    for i in range(1, len(values)):
        out = jnp.where(index == i, values[i], out)
    return out


def end_blocks(owned, plan_ref, own_ref, out_refs):
    copies = plan_ref.shape[1]
    rank = own_ref.shape[0] // owned
    group = lax.axis_index("store")
    end = jnp.where(group < 2, 0, 3)
    for l, place in enumerate(order_of(plan_ref, owned, end, 3 - end)):
        for block, out_ref in enumerate(out_refs):

            @pl.when(jnp.logical_and(place // copies == block, group == end))
            def _():
                at = pl.multiple_of((place % copies) * rank, rank)
                out_ref[pl.ds(at, rank), :] = own_ref[l * rank : (l + 1) * rank, :]

    for i in range(copies):

        @pl.when(group != end)
        def _():
            at = pl.multiple_of((plan_ref[end, i] % owned) * rank, rank)
            out_refs[0][i * rank : (i + 1) * rank, :] = own_ref[pl.ds(at, rank), :]


def end_blocks_kernel(owned, plan_ref, own_ref, low_ref, high_ref):
    end_blocks(owned, plan_ref, own_ref, (low_ref, high_ref))


def front_kernel(owned, plan_ref, own_ref, tokens_ref, target_ref, slot_ref, weight_ref, *refs):
    *refs, sems = refs
    low_ref, high_ref, sent_ref, *refs = refs
    copies = apart(weight_ref, sent_ref, sems)
    end_blocks(owned, plan_ref, own_ref, (low_ref, high_ref))
    sort_kernel(tokens_ref, target_ref, slot_ref, *refs)
    for copy in copies:
        copy.wait()


def apart(weight_ref, sent_ref, sems):
    width = weight_ref.shape[1]
    other = 1 - lax.axis_index("mp") % 2
    copies = []
    for q in range(sent_ref.shape[0] // width):
        start = pl.multiple_of((2 * q + other) * width, width)
        copies.append(
            pltpu.make_async_copy(
                weight_ref.at[pl.ds(start, width), :], sent_ref.at[pl.ds(q * width, width), :], sems.at[q]
            )
        )
    for copy in copies:
        copy.start()
    return copies


def pass_kernel(owned, dest_of, n_blocks, plan_ref, own_ref, *refs):
    out_ref = refs[-1]
    copies = plan_ref.shape[1]
    rank = own_ref.shape[0] // owned
    group = lax.axis_index("store")
    end = jnp.where(group < 2, 0, 3)
    places = order_of(plan_ref, owned, end, 3 - end)
    for i in range(copies):
        adapter = plan_ref[chosen(dest_of, group), i]
        owner, local = adapter // owned, adapter % owned
        at = slice(i * rank, (i + 1) * rank)

        @pl.when(owner == group)
        def _():
            out_ref[at, :] = own_ref[pl.ds(pl.multiple_of(local * rank, rank), rank), :]

        place = chosen(places, local)
        begin = pl.multiple_of((place % copies) * rank, rank)
        for j in range(n_blocks):

            @pl.when(jnp.logical_and(owner != group, place // copies == j))
            def _():
                out_ref[at, :] = refs[j][pl.ds(begin, rank), :]

        if n_blocks == 1:

            @pl.when(jnp.logical_and(owner != group, place // copies > 0))
            def _():
                out_ref[at, :] = refs[0][at, :]


def gather_kernel(owned, plan_ref, low_ref, high_ref, passed_ref, far_ref, out_ref):
    copies = plan_ref.shape[1]
    rank = out_ref.shape[0] // copies
    group = lax.axis_index("store")
    end = jnp.where(group < 2, 0, 3)
    beside = jnp.where(group < 2, 1, 2)
    places = order_of(plan_ref, owned, end, 3 - end)
    for i in range(copies):
        adapter = plan_ref[group, i]
        owner, local = adapter // owned, adapter % owned
        at = slice(i * rank, (i + 1) * rank)
        place = chosen(places, local)
        begin = pl.multiple_of((place % copies) * rank, rank)
        middle = group == beside

        def put(condition, value_of):
            @pl.when(condition)
            def _():
                out_ref[at, :] = value_of()

        raw = jnp.logical_and(middle, owner == end)
        put(jnp.logical_and(raw, place < copies), lambda: low_ref[pl.ds(begin, rank), :])
        put(jnp.logical_and(raw, place >= copies), lambda: high_ref[pl.ds(begin, rank), :])
        put(jnp.logical_and(middle, owner != end), lambda: passed_ref[at, :])
        put(jnp.logical_and(group == end, owner == beside), lambda: low_ref[at, :])
        put(jnp.logical_and(group == end, owner != beside), lambda: far_ref[at, :])


def apart_kernel(weight_ref, sent_ref, sems):
    for copy in apart(weight_ref, sent_ref, sems):
        copy.wait()


def two_parts(row):
    high = row.astype(BF16).astype(F32)
    at = iota((EXT, row.shape[1]), 0)
    return jnp.where(at == 0, high, jnp.where(at == 1, row - high, 0.0)).astype(BF16)


def put_extra(msg_ref, rows, inner, squares):
    width = msg_ref.shape[1]
    groups = 0 if inner is None else inner.shape[0] // EXT
    rank_groups = width // rows
    msg_ref[rows:, :] = jnp.zeros((EXT, width), BF16)
    for g in range(groups):
        msg_ref[rows:, g * rows : (g + 1) * rows] = inner[g * EXT : (g + 1) * EXT].astype(BF16)
    msg_ref[rows:, (rank_groups - 1) * rows :] = two_parts(squares)


def squares_row(state):
    total = jnp.sum(state * state, axis=1, keepdims=True)
    rows = state.shape[0]
    return jnp.transpose(jnp.broadcast_to(total, (rows, rows)))[0:1, :]


def slot_masks(slots, first, count, shape):
    return [jnp.broadcast_to(slots[0:1, :] == float(j), shape) for j in range(first, first + count)]


def inner_partial(u, slots, down_refs, rank):
    first, total = 0, None
    rows = u.shape[0]
    for ref in down_refs:
        count = ref.shape[0] // rank
        product = dot(ref[...], u, CONTRACT_LAST)
        for j, mask in enumerate(slot_masks(slots, first, count, (rank, rows))):
            term = jnp.where(mask, product[j * rank : (j + 1) * rank], 0.0)
            total = term if total is None else total + term
        first += count
    return total


def my_columns(gain_ref, width):
    return gain_ref[:, pl.ds(pl.multiple_of(lax.axis_index("mp") * width, width), width)]


def first_kernel(gain_ref, *refs):
    n = (len(refs) - 1) // 4
    chunk_refs, state_refs, slots_refs, msg_ref = refs[: 2 * n], refs[2 * n : 3 * n], refs[3 * n : 4 * n], refs[4 * n]
    for h in range(n):
        even_ref, odd_ref, state_ref, slots_ref = chunk_refs[2 * h], chunk_refs[2 * h + 1], state_refs[h], slots_refs[h]
        cap = even_ref.shape[0]
        rows, width = state_ref.shape
        state_ref[:cap] = even_ref[:, :width]
        state_ref[cap:] = odd_ref[:, :width]
        lane = iota((8, rows), 1)
        even, odd = even_ref[:, width:].astype(F32)[0:8], odd_ref[:, width:].astype(F32)[0:8]
        slots_ref[...] = jnp.where(lane < cap, even, odd) - 1.0
        state = state_ref[...].astype(F32)
        part_ref = msg_ref.at[h * (rows + EXT) : (h + 1) * (rows + EXT)]
        part_ref[:rows, :] = (state * my_columns(gain_ref, width)).astype(BF16)
        put_extra(part_ref, rows, None, squares_row(state))


def first_inner_kernel(msg_ref, slots0_ref, slots1_ref, own_ref, copy_ref, out_ref):
    rank, rows = out_ref.shape[0], out_ref.shape[1] // 2
    for h, slots in enumerate((slots0_ref, slots1_ref)):
        u = msg_ref[h * (rows + EXT) : h * (rows + EXT) + rows, :]
        out_ref[:, h * rows : (h + 1) * rows] = inner_partial(u, slots[...], (own_ref, copy_ref), rank)


def block_kernel(n_blocks, n_halves, at, last, weight_ref, other_ref, *refs):
    msgs, refs = refs[:n_blocks], refs[n_blocks:]
    width = weight_ref.shape[1]
    rows = msgs[0].shape[0] // n_halves - EXT
    if at[0] == 0:
        old = None
        outs = refs
    else:
        old, outs = refs[:3], refs[3:]
    mine = theirs = extra = None
    part = lax.axis_index("mp")
    core = part % 2

    def both(msg, under):
        parts = []
        for h in range(n_halves):
            begin = h * (rows + EXT)
            parts.append(msg[begin + rows : begin + rows + EXT, :] if under else msg[begin : begin + rows, :])
        return parts[0] if n_halves == 1 else jnp.concatenate(parts, axis=0)

    for i, msg in enumerate(msgs):
        q = jnp.bitwise_xor(part // 2, (0, 1 + core, 2 - core, 3)[at[i]])
        u = both(msg, False)
        a = dot(u, weight_ref[pl.ds(pl.multiple_of((2 * q + core) * width, width), width), :])
        b = dot(u, other_ref[pl.ds(pl.multiple_of(q * width, width), width), :])
        e = both(msg, True).astype(F32)
        mine, theirs, extra = (a, b, e) if mine is None else (mine + a, theirs + b, extra + e)
    if old is not None:
        mine, theirs, extra = mine + old[0][...], theirs + old[1][...], extra + old[2][...]
    outs[0][...] = mine
    outs[2][...] = extra
    if not last:
        outs[1][...] = theirs
        return
    for h in range(n_halves):
        begin = h * (rows + EXT)
        outs[1][begin : begin + rows, :] = theirs[h * rows : (h + 1) * rows].astype(BF16)
        under = extra[h * EXT : (h + 1) * EXT]
        outs[1][begin + rows : begin + rows + EXT, :] = under.astype(BF16)
        tail = under[:, width - rows :]
        outs[1][begin + rows : begin + rows + EXT, width - rows :] = two_parts(tail[0:1] + tail[1:2])


def finish_kernel(
    n_halves, h, last, rank, mine_ref, extra_ref, got_ref, state_ref, slots_ref, gain_ref, down_ref, downc_ref, up_ref, upc_ref, *refs
):
    rows, width = state_ref.shape
    width_all = gain_ref.shape[1]
    if n_halves > 1:
        inner_ref, refs = refs[0], refs[1:]
    begin = h * (rows + EXT)
    extra = extra_ref[h * EXT : (h + 1) * EXT, :] + got_ref[begin + rows : begin + rows + EXT, :].astype(F32)
    if n_halves > 1:
        inner = inner_ref[:, h * rows : (h + 1) * rows]
    else:
        inner = jnp.concatenate(
            [extra[:, g * rows : (g + 1) * rows] for g in range(rank // EXT)], axis=0
        )
    tail = extra[:, width - rows :]
    scale = lax.rsqrt((tail[0:1] + tail[1:2]) / width_all + EPS)
    inner = (inner * scale).astype(BF16).astype(F32)
    slots = slots_ref[...]
    outer, held = None, 0
    for ref in (up_ref, upc_ref):
        count = ref.shape[0] // rank
        spread = jnp.concatenate(
            [jnp.where(m, inner, 0.0) for m in slot_masks(slots, held, count, (rank, rows))], axis=0
        ).astype(BF16)
        term = dot(spread, ref[...], CONTRACT_FIRST)
        outer = term if outer is None else outer + term
        held += count
    delta = (adapter_scale * outer).astype(BF16).astype(F32)
    column = jnp.transpose(jnp.broadcast_to(scale, (rows, rows)))
    column = jnp.concatenate([column] * (width // rows), axis=1)
    base = (mine_ref[h * rows : (h + 1) * rows, :] + got_ref[begin : begin + rows, :].astype(F32)) * column
    state = (state_ref[...].astype(F32) + base + delta).astype(BF16)
    if last:
        refs[0][...] = state[: rows // 2]
        refs[1][...] = state[rows // 2 :]
        return
    refs[0][...] = state
    msg_ref = refs[1]
    state = state.astype(F32)
    u = (state * my_columns(gain_ref, width)).astype(BF16)
    msg_ref[:rows, :] = u
    put_extra(msg_ref, rows, inner_partial(u, slots, (down_ref, downc_ref), rank), squares_row(state))


def body(tokens, gain, base_projection_weight, adapter_down_weight, adapter_up_weight, plan, target, slot):
    groups = lax.axis_size("store")
    parts = lax.axis_size("mp")
    n_tokens, width = tokens.shape
    owned, rank = adapter_down_weight.shape[:2]
    rows = 2 * CAP
    gain = gain.reshape(1, parts * width)

    def mp(x, pairs_of):
        return lax.ppermute(x, "mp", [(i, pairs_of(i)) for i in range(parts)])

    def sibling(x):
        return mp(x, lambda i: i ^ 1)

    def side_a(x):
        return mp(x, lambda i: i ^ (4 if i % 2 else 2))

    def side_b(x):
        return mp(x, lambda i: i ^ (2 if i % 2 else 4))

    def store(x, k):
        return lax.ppermute(x, "store", [(g, g ^ k) for g in range(groups)])

    down = adapter_down_weight.reshape(owned * rank, width)
    up = adapter_up_weight.reshape(owned * rank, width)

    copies = plan.shape[1]
    shape = ((copies * rank, width), BF16)
    def pick(kernel, out, *args, name=None, after=()):
        return call(kernel, out, [IN_SMEM] + [IN_VMEM] * len(args), plan, *args, name=name, after=after)

    def line(x, pairs):
        return lax.ppermute(x, "store", pairs)

    def passing(dest_of, own, *blocks, name=None, after=()):
        kernel = functools.partial(pass_kernel, owned, dest_of, len(blocks))
        return pick(kernel, shape, own, *blocks, name=name, after=after)

    pairs, ends, middle, across = [(0, 1), (1, 0), (2, 3), (3, 2)], [(0, 1), (3, 2)], [(1, 2), (2, 1)], [(1, 3), (2, 0)]
    sent = ((parts // 2 * width, width), BF16)
    far_weight = pltpu.with_memory_space_constraint(base_projection_weight, pltpu.HBM)
    low0, high0, other, perm, *chunks = call(
        functools.partial(front_kernel, owned),
        [shape, shape, sent, ((groups * CAP, n_tokens), BF16)] + [((CAP, width + rows), BF16)] * groups,
        [IN_SMEM] + [IN_VMEM] * 4 + [pl.BlockSpec(memory_space=pl.ANY)],
        plan,
        *(
            pltpu.with_memory_space_constraint(x, pltpu.HBM)
            for x in (down, tokens, target.reshape(1, n_tokens), slot.reshape(1, n_tokens))
        ),
        far_weight,
        name="front",
        scratch=[pltpu.SemaphoreType.DMA((parts // 2,))],
    )
    low0 = line(low0, pairs)
    high0 = line(high0, ends)
    chunks = [c if k == 0 else store(c, k) for k, c in enumerate(chunks)]
    other = sibling(other)
    low1, high1 = pick(functools.partial(end_blocks_kernel, owned), [shape, shape], up, name="ends1", after=[low0, *chunks[1:]])
    low1 = line(low1, pairs)
    high1 = line(high1, ends)
    far0 = passing((3, 3, 0, 0), down, low0, name="far0")
    far0 = line(far0, across)
    pass0 = passing((2, 2, 1, 1), down, low0, high0, name="near0")
    pass0 = line(pass0, middle)
    far1 = line(passing((3, 3, 0, 0), up, low1, name="far1"), across)
    pass1 = line(passing((2, 2, 1, 1), up, low1, high1, name="near1"), middle)
    down_copy = pick(functools.partial(gather_kernel, owned), shape, low0, high0, pass0, far0, name="gather0")
    up_copy = pick(functools.partial(gather_kernel, owned), shape, low1, high1, pass1, far1, name="gather1")
    weight, other = pinned(base_projection_weight), pinned(other)

    halves = range(groups // 2)
    n = len(halves)
    acc = ((rows, width), F32)
    message = ((rows + EXT, width), BF16)

    def blocks_of(n_halves, msgs, at, old, last):
        many = [((n_halves * r, c), d) for (r, c), d in (acc, message if last else acc, ((EXT, width), F32))]
        return call(
            functools.partial(block_kernel, len(msgs), n_halves, at, last),
            many,
            [IN_VMEM] * (2 + len(msgs) + len(old)),
            weight,
            other,
            *msgs,
            *old,
            name="blocks",
        )

    def exchange(n_halves, msg):
        a = side_a(msg)
        b = side_b(msg)
        old = blocks_of(n_halves, [msg], (0,), (), False)
        d = side_b(a)
        old = blocks_of(n_halves, [a, b], (1, 2), old, False)
        mine, theirs, extra = blocks_of(n_halves, [d], (3,), old, True)
        return mine, extra, sibling(theirs)

    def finish(n_halves, h, final, sums, state, slots, inner=()):
        args = [*sums, state, slots, gain, down, down_copy, up, up_copy, *inner]
        return call(
            functools.partial(finish_kernel, n_halves, h, final, rank),
            [((CAP, width), BF16)] * 2 if final else [((rows, width), BF16), message],
            [IN_VMEM] * len(args),
            *args,
            name="finish",
        )

    outs = call(
        first_kernel,
        [((rows, width), BF16)] * n + [((8, rows), F32)] * n + [((n * (rows + EXT), width), BF16)],
        [IN_VMEM] * (1 + groups),
        gain,
        *chunks,
        name="first",
        after=[low0, other],
    )
    state, slots, msg = outs[:n], outs[n : 2 * n], outs[-1]
    sums = exchange(n, msg)
    inner = call(
        first_inner_kernel, ((rank, n * rows), F32), [IN_VMEM] * 5, msg, *slots, down, down_copy, name="first_inner"
    )
    for k in (2, 4, 1):
        inner = inner + mp(inner, lambda i: i ^ k)
    outs = [finish(n, h, False, sums, state[h], slots[h], [inner]) for h in halves]
    state, msg = [o[0] for o in outs], [o[1] for o in outs]
    for step in range(1, STEPS):
        final = step == STEPS - 1
        for h in halves:
            outs = finish(1, 0, final, exchange(1, msg[h]), state[h], slots[h])
            if final:
                state[h] = outs
            else:
                state[h], msg[h] = outs

    back = [c if k == 0 else store(c, k) for k, c in enumerate(sum(map(list, state), []))]
    return call(
        unsort_kernel,
        ((n_tokens, width), BF16),
        [IN_VMEM] * (1 + groups),
        perm,
        *back,
        name="unsort",
    )


def plain_body(
    tokens, gain, base_projection_weight, adapter_down_weight, adapter_up_weight, plan, target, slot
):
    store_count = lax.axis_size("store")
    group = lax.axis_index("store")
    owned_adapters, rank, width = adapter_down_weight.shape
    replica_count = plan.shape[1]
    n_slots = owned_adapters + replica_count
    owner = plan // owned_adapters
    local = plan % owned_adapters
    select = jnp.logical_and(
        (owner == group)[:, :, None],
        local[:, :, None] == jnp.arange(owned_adapters, dtype=jnp.int32)[None, None, :],
    )
    select = select.astype(BF16).reshape(store_count * replica_count, owned_adapters)

    def held(own):
        send = jnp.dot(select, own.reshape(owned_adapters, rank * width), preferred_element_type=F32)
        send = send.astype(BF16).reshape(store_count, replica_count, rank * width)
        got = lax.all_to_all(send, "store", split_axis=0, concat_axis=0, tiled=True)
        got = jnp.sum(got.astype(F32), axis=0).astype(BF16)
        both = jnp.concatenate([own, got.reshape(replica_count, rank, width)], 0)
        return both.reshape(n_slots * rank, width)

    host_down, host_up = held(adapter_down_weight), held(adapter_up_weight)
    target_group = target[:, 0]
    n_tokens = target_group.shape[0]
    member = (target_group[:, None] == jnp.arange(store_count, dtype=jnp.int32)[None, :]).astype(BF16)
    order = jnp.arange(n_tokens)
    before = (order[:, None] > order[None, :]).astype(BF16)
    earlier = jnp.dot(before, member, preferred_element_type=F32)
    place = jnp.sum(earlier * member.astype(F32), axis=1).astype(jnp.int32)
    row_index = target_group * CAP + place
    slots = jnp.full((store_count * CAP,), -1, jnp.int32).at[row_index].set(slot)
    state = jnp.zeros((store_count * CAP, width), BF16).at[row_index].set(tokens)

    def exchange(x):
        return lax.all_to_all(
            x.reshape(store_count, CAP, -1), "store", split_axis=0, concat_axis=0, tiled=True
        ).reshape(store_count * CAP, -1)

    state = exchange(state)
    selected = exchange(slots) == jnp.arange(n_slots, dtype=jnp.int32)[None, :]
    total_rows = state.shape[0]
    column_start = lax.axis_index("mp") * width
    for step in range(STEPS):
        whole = lax.all_gather(state, "mp", axis=1, tiled=True)
        values = whole.astype(F32)
        mean_sq = jnp.mean(values * values, axis=1, keepdims=True)
        normed = (values * lax.rsqrt(mean_sq + EPS) * gain[None, :]).astype(BF16)
        mine = lax.dynamic_slice_in_dim(normed, column_start, width, 1)
        partial_value = lax.dot_general(mine, host_down, CONTRACT_LAST, preferred_element_type=F32)
        partial_value = jnp.sum(
            partial_value.reshape(total_rows, n_slots, rank) * selected[:, :, None].astype(F32), axis=1
        )
        inner = lax.psum(partial_value, "mp").astype(BF16)
        spread = (selected[:, :, None].astype(BF16) * inner[:, None, :]).reshape(total_rows, -1)
        outer = jnp.dot(spread, host_up, preferred_element_type=F32)
        delta = (adapter_scale * outer).astype(BF16).astype(F32)
        base = jnp.dot(normed, base_projection_weight, preferred_element_type=F32)
        state = (state.astype(F32) + base + delta).astype(BF16)
    return exchange(state)[row_index]


def solution(mesh):
    parts, groups = mesh.shape["mp"], mesh.shape["store"]

    def run(tokens, *rest):
        width = tokens.shape[1] // parts
        rank = rest[2].shape[1]
        rows = 2 * CAP
        cube = parts == 8 and groups == 4
        cube = cube and rest[2].shape[0] == 2 * groups * rest[4].shape[1]
        fits = rank % EXT == 0 and width % rows == 0 and rank // EXT + 1 <= width // rows
        return jax.shard_map(
            body if cube and fits else plain_body,
            mesh=mesh,
            in_specs=(
                P("store", "mp"),
                P(),
                P(None, "mp"),
                P("store", None, "mp"),
                P("store", None, "mp"),
                P(),
                P("store", None),
                P("store"),
            ),
            out_specs=P("store", "mp"),
            check_vma=False,
        )(tokens, *rest)

    return run
```

```python
import functools
import math

import jax
import jax.numpy as jnp
from jax import lax
from jax.experimental import pallas as pl
from jax.experimental.pallas import tpu as pltpu
from jax.sharding import PartitionSpec as P

STEPS = 4
CAP = 64
EPS = 1e-05
EXT = 16
MIB = 2**20

adapter_scale = 0.5
ORDER_US = {'near1': 5, 'far1': 5, 'ends1': 10, 'first': 20}

F32 = jnp.float32
BF16 = jnp.bfloat16
IN_VMEM = pl.BlockSpec(memory_space=pltpu.VMEM)
IN_SMEM = pl.BlockSpec(memory_space=pltpu.SMEM)
CONTRACT_LAST = (((1,), (1,)), ((), ()))
CONTRACT_FIRST = (((0,), (0,)), ((), ()))


def pinned(x):
    return pltpu.with_memory_space_constraint(x, pltpu.VMEM)


def call(kernel, out, specs, *args, name=None, scratch=(), pin=False, after=()):
    many = isinstance(out, list)
    n_args, kernel_of = len(args), kernel
    if after:
        args, specs = (*args, *after), [*specs] + [pl.BlockSpec(memory_space=pl.ANY)] * len(after)

        def kernel(*refs):
            kernel_of(*refs[:n_args], *refs[n_args + len(after) :])

    kind = pltpu.VMEM if pin else jax.ShapeDtypeStruct
    shapes = [kind(s, d) for s, d in (out if many else [out])]
    r = pl.pallas_call(
        kernel,
        out_shape=shapes,
        in_specs=specs,
        out_specs=[IN_VMEM] * len(shapes),
        scratch_shapes=scratch,
        compiler_params=pltpu.CompilerParams(vmem_limit_bytes=12 * MIB),
        cost_estimate=pl.CostEstimate(flops=int(ORDER_US.get(name, 0) * 1.15e9), bytes_accessed=0, transcendentals=0),
        name=name,
    )(*args)
    return r if many else r[0]


def dot(a, b, dims=(((1,), (0,)), ((), ()))):
    return lax.dot_general(a, b, dims, preferred_element_type=F32)


def iota(shape, dim):
    return lax.broadcasted_iota(jnp.int32, shape, dim)


def sort_kernel(tokens_ref, target_ref, slot_ref, perm_ref, *chunk_refs):
    n_tokens, width = tokens_ref.shape
    groups = len(chunk_refs)
    rows = groups * CAP
    apart = jnp.bitwise_xor(target_ref[...], lax.axis_index("store"))
    member = (iota((max(8, groups), n_tokens), 0) == apart).astype(F32)
    before = (iota((n_tokens, n_tokens), 0) < iota((n_tokens, n_tokens), 1)).astype(BF16)
    earlier = dot(member.astype(BF16), before)
    place = jnp.sum(earlier * member, axis=0, keepdims=True).astype(jnp.int32)
    perm = (iota((rows, n_tokens), 0) == apart * CAP + place).astype(F32).astype(BF16)
    perm_ref[...] = perm
    sorted_rows = dot(perm, tokens_ref[...]).astype(BF16)
    slots = jnp.broadcast_to((slot_ref[...] + 1).astype(F32), (8, n_tokens)).astype(BF16)
    slots = dot(slots, perm, CONTRACT_LAST)
    lanes = 2 * CAP
    for k, ref in enumerate(chunk_refs):
        ref[:, :width] = sorted_rows[k * CAP : (k + 1) * CAP]
        half = slots[:, (k // 2) * lanes : (k // 2 + 1) * lanes]
        ref[:, width:] = jnp.concatenate([half, jnp.zeros((CAP - 8, lanes), F32)], 0).astype(BF16)


def unsort_kernel(perm_ref, *refs):
    rows = jnp.concatenate([r[...] for r in refs[:-1]], axis=0)
    refs[-1][...] = dot(perm_ref[...], rows, CONTRACT_FIRST).astype(BF16)


def order_of(plan_ref, owned, end, far):
    asked = []
    for l in range(owned):
        hit = [plan_ref[far, i] == end * owned + l for i in range(plan_ref.shape[1])]
        asked.append(functools.reduce(jnp.logical_or, hit).astype(jnp.int32))
    total, seen, places = sum(asked), 0, []
    for l in range(owned):
        places.append(jnp.where(asked[l] == 1, seen, total + l - seen))
        seen = seen + asked[l]
    return places


def chosen(values, index):
    out = values[0]
    for i in range(1, len(values)):
        out = jnp.where(index == i, values[i], out)
    return out


def end_blocks(owned, plan_ref, own_ref, out_refs):
    copies = plan_ref.shape[1]
    rank = own_ref.shape[0] // owned
    group = lax.axis_index("store")
    end = jnp.where(group < 2, 0, 3)
    for l, place in enumerate(order_of(plan_ref, owned, end, 3 - end)):
        for block, out_ref in enumerate(out_refs):

            @pl.when(jnp.logical_and(place // copies == block, group == end))
            def _():
                at = pl.multiple_of((place % copies) * rank, rank)
                out_ref[pl.ds(at, rank), :] = own_ref[l * rank : (l + 1) * rank, :]

    for i in range(copies):

        @pl.when(group != end)
        def _():
            at = pl.multiple_of((plan_ref[end, i] % owned) * rank, rank)
            out_refs[0][i * rank : (i + 1) * rank, :] = own_ref[pl.ds(at, rank), :]


def end_blocks_kernel(owned, plan_ref, own_ref, low_ref, high_ref):
    end_blocks(owned, plan_ref, own_ref, (low_ref, high_ref))


def front_kernel(owned, plan_ref, own_ref, tokens_ref, target_ref, slot_ref, weight_ref, *refs):
    *refs, sems = refs
    low_ref, high_ref, sent_ref, *refs = refs
    copies = apart(weight_ref, sent_ref, sems)
    end_blocks(owned, plan_ref, own_ref, (low_ref, high_ref))
    sort_kernel(tokens_ref, target_ref, slot_ref, *refs)
    for copy in copies:
        copy.wait()


def apart(weight_ref, sent_ref, sems):
    width = weight_ref.shape[1]
    other = 1 - lax.axis_index("mp") % 2
    copies = []
    for q in range(sent_ref.shape[0] // width):
        start = pl.multiple_of((2 * q + other) * width, width)
        copies.append(
            pltpu.make_async_copy(
                weight_ref.at[pl.ds(start, width), :], sent_ref.at[pl.ds(q * width, width), :], sems.at[q]
            )
        )
    for copy in copies:
        copy.start()
    return copies


def pass_kernel(owned, dest_of, n_blocks, plan_ref, own_ref, *refs):
    out_ref = refs[-1]
    copies = plan_ref.shape[1]
    rank = own_ref.shape[0] // owned
    group = lax.axis_index("store")
    end = jnp.where(group < 2, 0, 3)
    places = order_of(plan_ref, owned, end, 3 - end)
    for i in range(copies):
        adapter = plan_ref[chosen(dest_of, group), i]
        owner, local = adapter // owned, adapter % owned
        at = slice(i * rank, (i + 1) * rank)

        @pl.when(owner == group)
        def _():
            out_ref[at, :] = own_ref[pl.ds(pl.multiple_of(local * rank, rank), rank), :]

        place = chosen(places, local)
        begin = pl.multiple_of((place % copies) * rank, rank)
        for j in range(n_blocks):

            @pl.when(jnp.logical_and(owner != group, place // copies == j))
            def _():
                out_ref[at, :] = refs[j][pl.ds(begin, rank), :]

        if n_blocks == 1:

            @pl.when(jnp.logical_and(owner != group, place // copies > 0))
            def _():
                out_ref[at, :] = refs[0][at, :]


def gather_kernel(owned, plan_ref, low_ref, high_ref, passed_ref, far_ref, out_ref):
    copies = plan_ref.shape[1]
    rank = out_ref.shape[0] // copies
    group = lax.axis_index("store")
    end = jnp.where(group < 2, 0, 3)
    beside = jnp.where(group < 2, 1, 2)
    places = order_of(plan_ref, owned, end, 3 - end)
    for i in range(copies):
        adapter = plan_ref[group, i]
        owner, local = adapter // owned, adapter % owned
        at = slice(i * rank, (i + 1) * rank)
        place = chosen(places, local)
        begin = pl.multiple_of((place % copies) * rank, rank)
        middle = group == beside

        def put(condition, value_of):
            @pl.when(condition)
            def _():
                out_ref[at, :] = value_of()

        raw = jnp.logical_and(middle, owner == end)
        put(jnp.logical_and(raw, place < copies), lambda: low_ref[pl.ds(begin, rank), :])
        put(jnp.logical_and(raw, place >= copies), lambda: high_ref[pl.ds(begin, rank), :])
        put(jnp.logical_and(middle, owner != end), lambda: passed_ref[at, :])
        put(jnp.logical_and(group == end, owner == beside), lambda: low_ref[at, :])
        put(jnp.logical_and(group == end, owner != beside), lambda: far_ref[at, :])


def apart_kernel(weight_ref, sent_ref, sems):
    for copy in apart(weight_ref, sent_ref, sems):
        copy.wait()


def tie(x, deps):
    return lax.optimization_barrier((x, *deps))[0] if deps else x


def two_parts(row):
    high = row.astype(BF16).astype(F32)
    at = iota((EXT, row.shape[1]), 0)
    return jnp.where(at == 0, high, jnp.where(at == 1, row - high, 0.0)).astype(BF16)


def put_extra(msg_ref, rows, inner, squares):
    width = msg_ref.shape[1]
    groups = 0 if inner is None else inner.shape[0] // EXT
    rank_groups = width // rows
    msg_ref[rows:, :] = jnp.zeros((EXT, width), BF16)
    for g in range(groups):
        msg_ref[rows:, g * rows : (g + 1) * rows] = inner[g * EXT : (g + 1) * EXT].astype(BF16)
    msg_ref[rows:, (rank_groups - 1) * rows :] = two_parts(squares)


def squares_row(state):
    total = jnp.sum(state * state, axis=1, keepdims=True)
    rows = state.shape[0]
    return jnp.transpose(jnp.broadcast_to(total, (rows, rows)))[0:1, :]


def slot_masks(slots, first, count, shape):
    return [jnp.broadcast_to(slots[0:1, :] == float(j), shape) for j in range(first, first + count)]


def inner_partial(u, slots, down_refs, rank):
    first, total = 0, None
    rows = u.shape[0]
    for ref in down_refs:
        count = ref.shape[0] // rank
        product = dot(ref[...], u, CONTRACT_LAST)
        for j, mask in enumerate(slot_masks(slots, first, count, (rank, rows))):
            term = jnp.where(mask, product[j * rank : (j + 1) * rank], 0.0)
            total = term if total is None else total + term
        first += count
    return total


def my_columns(gain_ref, width):
    return gain_ref[:, pl.ds(pl.multiple_of(lax.axis_index("mp") * width, width), width)]


def first_kernel(gain_ref, *refs):
    n = (len(refs) - 1) // 4
    chunk_refs, state_refs, slots_refs, msg_ref = refs[: 2 * n], refs[2 * n : 3 * n], refs[3 * n : 4 * n], refs[4 * n]
    for h in range(n):
        even_ref, odd_ref, state_ref, slots_ref = chunk_refs[2 * h], chunk_refs[2 * h + 1], state_refs[h], slots_refs[h]
        cap = even_ref.shape[0]
        rows, width = state_ref.shape
        state_ref[:cap] = even_ref[:, :width]
        state_ref[cap:] = odd_ref[:, :width]
        lane = iota((8, rows), 1)
        even, odd = even_ref[:, width:].astype(F32)[0:8], odd_ref[:, width:].astype(F32)[0:8]
        slots_ref[...] = jnp.where(lane < cap, even, odd) - 1.0
        state = state_ref[...].astype(F32)
        part_ref = msg_ref.at[h * (rows + EXT) : (h + 1) * (rows + EXT)]
        part_ref[:rows, :] = (state * my_columns(gain_ref, width)).astype(BF16)
        put_extra(part_ref, rows, None, squares_row(state))


def first_inner_kernel(msg_ref, slots0_ref, slots1_ref, own_ref, copy_ref, out_ref):
    rank, rows = out_ref.shape[0], out_ref.shape[1] // 2
    for h, slots in enumerate((slots0_ref, slots1_ref)):
        u = msg_ref[h * (rows + EXT) : h * (rows + EXT) + rows, :]
        out_ref[:, h * rows : (h + 1) * rows] = inner_partial(u, slots[...], (own_ref, copy_ref), rank)


def block_kernel(n_blocks, n_halves, at, last, weight_ref, other_ref, *refs):
    msgs, refs = refs[:n_blocks], refs[n_blocks:]
    width = weight_ref.shape[1]
    rows = msgs[0].shape[0] // n_halves - EXT
    if at[0] == 0:
        old = None
        outs = refs
    else:
        old, outs = refs[:3], refs[3:]
    mine = theirs = extra = None
    part = lax.axis_index("mp")
    core = part % 2

    def both(msg, under):
        parts = []
        for h in range(n_halves):
            begin = h * (rows + EXT)
            parts.append(msg[begin + rows : begin + rows + EXT, :] if under else msg[begin : begin + rows, :])
        return parts[0] if n_halves == 1 else jnp.concatenate(parts, axis=0)

    for i, msg in enumerate(msgs):
        q = jnp.bitwise_xor(part // 2, (0, 1 + core, 2 - core, 3)[at[i]])
        u = both(msg, False)
        a = dot(u, weight_ref[pl.ds(pl.multiple_of((2 * q + core) * width, width), width), :])
        b = dot(u, other_ref[pl.ds(pl.multiple_of(q * width, width), width), :])
        e = both(msg, True).astype(F32)
        mine, theirs, extra = (a, b, e) if mine is None else (mine + a, theirs + b, extra + e)
    if old is not None:
        mine, theirs, extra = mine + old[0][...], theirs + old[1][...], extra + old[2][...]
    outs[0][...] = mine
    outs[2][...] = extra
    if not last:
        outs[1][...] = theirs
        return
    for h in range(n_halves):
        begin = h * (rows + EXT)
        outs[1][begin : begin + rows, :] = theirs[h * rows : (h + 1) * rows].astype(BF16)
        under = extra[h * EXT : (h + 1) * EXT]
        outs[1][begin + rows : begin + rows + EXT, :] = under.astype(BF16)
        tail = under[:, width - rows :]
        outs[1][begin + rows : begin + rows + EXT, width - rows :] = two_parts(tail[0:1] + tail[1:2])


def finish_kernel(
    n_halves, h, last, rank, mine_ref, extra_ref, got_ref, state_ref, slots_ref, gain_ref, down_ref, downc_ref, up_ref, upc_ref, *refs
):
    rows, width = state_ref.shape
    width_all = gain_ref.shape[1]
    if n_halves > 1:
        inner_ref, refs = refs[0], refs[1:]
    begin = h * (rows + EXT)
    extra = extra_ref[h * EXT : (h + 1) * EXT, :] + got_ref[begin + rows : begin + rows + EXT, :].astype(F32)
    if n_halves > 1:
        inner = inner_ref[:, h * rows : (h + 1) * rows]
    else:
        inner = jnp.concatenate(
            [extra[:, g * rows : (g + 1) * rows] for g in range(rank // EXT)], axis=0
        )
    tail = extra[:, width - rows :]
    scale = lax.rsqrt((tail[0:1] + tail[1:2]) / width_all + EPS)
    inner = (inner * scale).astype(BF16).astype(F32)
    slots = slots_ref[...]
    outer, held = None, 0
    for ref in (up_ref, upc_ref):
        count = ref.shape[0] // rank
        spread = jnp.concatenate(
            [jnp.where(m, inner, 0.0) for m in slot_masks(slots, held, count, (rank, rows))], axis=0
        ).astype(BF16)
        term = dot(spread, ref[...], CONTRACT_FIRST)
        outer = term if outer is None else outer + term
        held += count
    delta = (adapter_scale * outer).astype(BF16).astype(F32)
    column = jnp.transpose(jnp.broadcast_to(scale, (rows, rows)))
    column = jnp.concatenate([column] * (width // rows), axis=1)
    base = (mine_ref[h * rows : (h + 1) * rows, :] + got_ref[begin : begin + rows, :].astype(F32)) * column
    state = (state_ref[...].astype(F32) + base + delta).astype(BF16)
    if last:
        refs[0][...] = state[: rows // 2]
        refs[1][...] = state[rows // 2 :]
        return
    refs[0][...] = state
    msg_ref = refs[1]
    state = state.astype(F32)
    u = (state * my_columns(gain_ref, width)).astype(BF16)
    msg_ref[:rows, :] = u
    put_extra(msg_ref, rows, inner_partial(u, slots, (down_ref, downc_ref), rank), squares_row(state))


def body(tokens, gain, base_projection_weight, adapter_down_weight, adapter_up_weight, plan, target, slot):
    groups = lax.axis_size("store")
    parts = lax.axis_size("mp")
    n_tokens, width = tokens.shape
    owned, rank = adapter_down_weight.shape[:2]
    rows = 2 * CAP
    gain = gain.reshape(1, parts * width)

    def mp(x, pairs_of):
        return lax.ppermute(x, "mp", [(i, pairs_of(i)) for i in range(parts)])

    def sibling(x):
        return mp(x, lambda i: i ^ 1)

    def side_a(x):
        return mp(x, lambda i: i ^ (4 if i % 2 else 2))

    def side_b(x):
        return mp(x, lambda i: i ^ (2 if i % 2 else 4))

    def store(x, k):
        return lax.ppermute(x, "store", [(g, g ^ k) for g in range(groups)])

    down = adapter_down_weight.reshape(owned * rank, width)
    up = adapter_up_weight.reshape(owned * rank, width)

    copies = plan.shape[1]
    shape = ((copies * rank, width), BF16)
    def pick(kernel, out, *args, name=None, after=()):
        return call(kernel, out, [IN_SMEM] + [IN_VMEM] * len(args), plan, *args, name=name, after=after)

    def line(x, pairs):
        return lax.ppermute(x, "store", pairs)

    def passing(dest_of, own, *blocks, name=None, after=()):
        kernel = functools.partial(pass_kernel, owned, dest_of, len(blocks))
        return pick(kernel, shape, own, *blocks, name=name, after=after)

    pairs, ends, middle, across = [(0, 1), (1, 0), (2, 3), (3, 2)], [(0, 1), (3, 2)], [(1, 2), (2, 1)], [(1, 3), (2, 0)]
    sent = ((parts // 2 * width, width), BF16)
    far_weight = pltpu.with_memory_space_constraint(base_projection_weight, pltpu.HBM)
    low0, high0, other, perm, *chunks = call(
        functools.partial(front_kernel, owned),
        [shape, shape, sent, ((groups * CAP, n_tokens), BF16)] + [((CAP, width + rows), BF16)] * groups,
        [IN_SMEM] + [IN_VMEM] * 4 + [pl.BlockSpec(memory_space=pl.ANY)],
        plan,
        *(
            pltpu.with_memory_space_constraint(x, pltpu.HBM)
            for x in (down, tokens, target.reshape(1, n_tokens), slot.reshape(1, n_tokens))
        ),
        far_weight,
        name="front",
        scratch=[pltpu.SemaphoreType.DMA((parts // 2,))],
    )
    low0 = line(low0, pairs)
    high0 = line(high0, ends)
    chunks = [c if k == 0 else store(c, k) for k, c in enumerate(chunks)]
    other = sibling(other)
    low1, high1 = pick(functools.partial(end_blocks_kernel, owned), [shape, shape], up, name="ends1", after=[low0, *chunks[1:]])
    far0 = passing((3, 3, 0, 0), down, low0, name="far0")
    far0 = line(far0, across)
    pass0 = passing((2, 2, 1, 1), down, low0, high0, name="near0")
    pass0 = line(pass0, middle)
    low1 = line(low1, pairs)
    high1 = line(tie(high1, [far0]), ends)
    far1 = line(passing((3, 3, 0, 0), up, low1, name="far1"), across)
    pass1 = line(passing((2, 2, 1, 1), up, low1, high1, name="near1"), middle)
    down_copy = pick(functools.partial(gather_kernel, owned), shape, low0, high0, pass0, far0, name="gather0")
    up_copy = pick(functools.partial(gather_kernel, owned), shape, low1, high1, pass1, far1, name="gather1")
    weight, other = pinned(base_projection_weight), pinned(other)

    halves = range(groups // 2)
    n = len(halves)
    acc = ((rows, width), F32)
    message = ((rows + EXT, width), BF16)

    def blocks_of(n_halves, msgs, at, old, last):
        many = [((n_halves * r, c), d) for (r, c), d in (acc, message if last else acc, ((EXT, width), F32))]
        return call(
            functools.partial(block_kernel, len(msgs), n_halves, at, last),
            many,
            [IN_VMEM] * (2 + len(msgs) + len(old)),
            weight,
            other,
            *msgs,
            *old,
            name="blocks",
        )

    def exchange(n_halves, msg):
        a = side_a(msg)
        b = side_b(msg)
        old = blocks_of(n_halves, [msg], (0,), (), False)
        d = side_b(a)
        old = blocks_of(n_halves, [a, b], (1, 2), old, False)
        mine, theirs, extra = blocks_of(n_halves, [d], (3,), old, True)
        return mine, extra, sibling(theirs)

    def finish(n_halves, h, final, sums, state, slots, inner=()):
        args = [*sums, state, slots, gain, down, down_copy, up, up_copy, *inner]
        return call(
            functools.partial(finish_kernel, n_halves, h, final, rank),
            [((CAP, width), BF16)] * 2 if final else [((rows, width), BF16), message],
            [IN_VMEM] * len(args),
            *args,
            name="finish",
        )

    outs = call(
        first_kernel,
        [((rows, width), BF16)] * n + [((8, rows), F32)] * n + [((n * (rows + EXT), width), BF16)],
        [IN_VMEM] * (1 + groups),
        gain,
        *chunks,
        name="first",
        after=[low0, other],
    )
    state, slots, msg = outs[:n], outs[n : 2 * n], outs[-1]
    sums = exchange(n, msg)
    inner = call(
        first_inner_kernel, ((rank, n * rows), F32), [IN_VMEM] * 5, msg, *slots, down, down_copy, name="first_inner"
    )
    for k in (2, 4, 1):
        inner = inner + mp(inner, lambda i: i ^ k)
    outs = [finish(n, h, False, sums, state[h], slots[h], [inner]) for h in halves]
    state, msg = [o[0] for o in outs], [o[1] for o in outs]
    for step in range(1, STEPS):
        final = step == STEPS - 1
        for h in halves:
            outs = finish(1, 0, final, exchange(1, msg[h]), state[h], slots[h])
            if final:
                state[h] = outs
            else:
                state[h], msg[h] = outs

    back = [c if k == 0 else store(c, k) for k, c in enumerate(sum(map(list, state), []))]
    return call(
        unsort_kernel,
        ((n_tokens, width), BF16),
        [IN_VMEM] * (1 + groups),
        perm,
        *back,
        name="unsort",
    )


def plain_body(
    tokens, gain, base_projection_weight, adapter_down_weight, adapter_up_weight, plan, target, slot
):
    store_count = lax.axis_size("store")
    group = lax.axis_index("store")
    owned_adapters, rank, width = adapter_down_weight.shape
    replica_count = plan.shape[1]
    n_slots = owned_adapters + replica_count
    owner = plan // owned_adapters
    local = plan % owned_adapters
    select = jnp.logical_and(
        (owner == group)[:, :, None],
        local[:, :, None] == jnp.arange(owned_adapters, dtype=jnp.int32)[None, None, :],
    )
    select = select.astype(BF16).reshape(store_count * replica_count, owned_adapters)

    def held(own):
        send = jnp.dot(select, own.reshape(owned_adapters, rank * width), preferred_element_type=F32)
        send = send.astype(BF16).reshape(store_count, replica_count, rank * width)
        got = lax.all_to_all(send, "store", split_axis=0, concat_axis=0, tiled=True)
        got = jnp.sum(got.astype(F32), axis=0).astype(BF16)
        both = jnp.concatenate([own, got.reshape(replica_count, rank, width)], 0)
        return both.reshape(n_slots * rank, width)

    host_down, host_up = held(adapter_down_weight), held(adapter_up_weight)
    target_group = target[:, 0]
    n_tokens = target_group.shape[0]
    member = (target_group[:, None] == jnp.arange(store_count, dtype=jnp.int32)[None, :]).astype(BF16)
    order = jnp.arange(n_tokens)
    before = (order[:, None] > order[None, :]).astype(BF16)
    earlier = jnp.dot(before, member, preferred_element_type=F32)
    place = jnp.sum(earlier * member.astype(F32), axis=1).astype(jnp.int32)
    row_index = target_group * CAP + place
    slots = jnp.full((store_count * CAP,), -1, jnp.int32).at[row_index].set(slot)
    state = jnp.zeros((store_count * CAP, width), BF16).at[row_index].set(tokens)

    def exchange(x):
        return lax.all_to_all(
            x.reshape(store_count, CAP, -1), "store", split_axis=0, concat_axis=0, tiled=True
        ).reshape(store_count * CAP, -1)

    state = exchange(state)
    selected = exchange(slots) == jnp.arange(n_slots, dtype=jnp.int32)[None, :]
    total_rows = state.shape[0]
    column_start = lax.axis_index("mp") * width
    for step in range(STEPS):
        whole = lax.all_gather(state, "mp", axis=1, tiled=True)
        values = whole.astype(F32)
        mean_sq = jnp.mean(values * values, axis=1, keepdims=True)
        normed = (values * lax.rsqrt(mean_sq + EPS) * gain[None, :]).astype(BF16)
        mine = lax.dynamic_slice_in_dim(normed, column_start, width, 1)
        partial_value = lax.dot_general(mine, host_down, CONTRACT_LAST, preferred_element_type=F32)
        partial_value = jnp.sum(
            partial_value.reshape(total_rows, n_slots, rank) * selected[:, :, None].astype(F32), axis=1
        )
        inner = lax.psum(partial_value, "mp").astype(BF16)
        spread = (selected[:, :, None].astype(BF16) * inner[:, None, :]).reshape(total_rows, -1)
        outer = jnp.dot(spread, host_up, preferred_element_type=F32)
        delta = (adapter_scale * outer).astype(BF16).astype(F32)
        base = jnp.dot(normed, base_projection_weight, preferred_element_type=F32)
        state = (state.astype(F32) + base + delta).astype(BF16)
    return exchange(state)[row_index]


def solution(mesh):
    parts, groups = mesh.shape["mp"], mesh.shape["store"]

    def run(tokens, *rest):
        width = tokens.shape[1] // parts
        rank = rest[2].shape[1]
        rows = 2 * CAP
        cube = parts == 8 and groups == 4
        cube = cube and rest[2].shape[0] == 2 * groups * rest[4].shape[1]
        fits = rank % EXT == 0 and width % rows == 0 and rank // EXT + 1 <= width // rows
        return jax.shard_map(
            body if cube and fits else plain_body,
            mesh=mesh,
            in_specs=(
                P("store", "mp"),
                P(),
                P(None, "mp"),
                P("store", None, "mp"),
                P("store", None, "mp"),
                P(),
                P("store", None),
                P("store"),
            ),
            out_specs=P("store", "mp"),
            check_vma=False,
        )(tokens, *rest)

    return run
```
